256 devices in a mesh: frame: 64 (over x, z, y_hi), patch: 4 (over y_lo, core).
Axes of the slice: x: 4, y: 4 (y_hi: 2, y_lo: 2; y = y_hi * 2 + y_lo), z: 8, core: 2. Of those that a mesh axis runs over, the one named last changes fastest.
Arguments:
- hidden_in: bfloat16 [128, 512, 1152], P('frame', 'patch'), may hold values from -24 to 24
- grad_out: bfloat16 [128, 512, 1152], P('frame', 'patch'), may hold values from -6 to 6
- w_qkv: bfloat16 [1152, 3456], replicated, may hold values from -0.1875 to 0.1875
- w_out: bfloat16 [1152, 1152], replicated, may hold values from -0.1875 to 0.1875
Outputs:
- grad_in: bfloat16 [128, 512, 1152], P('frame', 'patch')
- grad_wqkv: float32 [1152, 3456], P('frame', 'patch')
- grad_wout: float32 [1152, 1152], P('frame', 'patch')
The draws below stay inside these ranges and needn't reach their ends.
All inputs are finite; a program needn't handle non-finite values.
Results may differ from the reference program's by a relative error of at most 0.015.
The reference program's roundings to bfloat16 on the way (of `qkv`, `dout`, `probs_b`, `attn`, `dscore` and `dqkv`) count: a program that leaves them out, or rounds other values in their place, can miss the bound.
Values may be sent and summed in bfloat16 or wider, within the bound.
No kernel may reach another device: no remote copies, remote signals or barrier semaphores. Data moves between devices by JAX's collectives and lax.ppermute only.
A program may use at most 128 MiB of HBM per device.

```python
import jax
import jax.numpy as jnp
from jax import lax

HEADS = 16
HD = 72
D = 1152
FRAMES = 128
PATCHES = 512


def draw_hidden_in(key, part):
    key = jax.random.fold_in(key, 11)
    base_key = jax.random.fold_in(key, 0)
    base = jax.random.truncated_normal(base_key, -6.0, 6.0, (FRAMES, PATCHES, D), jnp.float32)
    values = base
    return values.astype(jnp.bfloat16)


def levels(own_key, extent, cuts, smallest, largest):
    def one(position, blocks):
        draws = jax.random.uniform(jax.random.fold_in(jax.random.fold_in(own_key, 6), position), (blocks,), jnp.float32, smallest / len(cuts), largest / len(cuts))
        return jnp.repeat(jnp.exp(draws), extent[position] // blocks).reshape((-1,) + (1,) * (len(extent) - position - 1))

    level = one(*cuts[0])
    for cut in cuts[1:]:
        level = level * one(*cut)
    return level


def bell_draw(own_key, shape, scale, bound, pieces=(), dtype=jnp.bfloat16):
    result = jax.random.normal(own_key, shape, jnp.float32) * scale
    if len(pieces) > 0:
        result = levels(own_key, shape, pieces, -0.22, 0.18) * result
    return jnp.clip(result, min=-bound, max=bound).astype(dtype)


def setup_inputs(seed: int = 0) -> dict:
    splits = jax.random.split(jax.random.key(seed), 5)
    return {
        "hidden_in": draw_hidden_in(jax.random.fold_in(splits[4], 71), 0),
        "grad_out": bell_draw(splits[1], (FRAMES, PATCHES, D), 1.0, 6.0, ((0, 64), (1, 4))),
        "w_qkv": bell_draw(splits[2], (D, 3 * D), D ** -0.5, 0.1875),
        "w_out": bell_draw(splits[3], (D, D), D ** -0.5, 0.1875),
    }


def attend_block(block):
    qkv_b, dout_b = block
    frames, count, cols = qkv_b.shape
    width = cols // 3
    q = qkv_b[..., :width].reshape(frames, count, HEADS, HD).astype(jnp.float32)
    k = qkv_b[..., width:2 * width].reshape(frames, count, HEADS, HD).astype(jnp.float32)
    v = qkv_b[..., 2 * width:].reshape(frames, count, HEADS, HD).astype(jnp.float32)
    dout = dout_b.reshape(frames, count, HEADS, HD).astype(jnp.float32)
    scale = 1.0 / (HD ** 0.5)
    scores = jnp.einsum("fphd,gphd->phfg", q, k) * scale
    probs = jax.nn.softmax(scores, axis=-1)
    probs_b = probs.astype(jnp.bfloat16)
    pf = probs_b.astype(jnp.float32)
    attn = jnp.einsum("phfg,gphd->fphd", pf, v).astype(jnp.bfloat16)
    dprob = jnp.einsum("fphd,gphd->phfg", dout, v)
    dscore = (probs * (dprob - jnp.sum(probs * dprob, axis=-1, keepdims=True)) * scale).astype(jnp.bfloat16)
    dsf = dscore.astype(jnp.float32)
    dq = jnp.einsum("phfg,gphd->fphd", dsf, k).astype(jnp.bfloat16)
    dk = jnp.einsum("phfg,fphd->gphd", dsf, q).astype(jnp.bfloat16)
    dv = jnp.einsum("phfg,fphd->gphd", pf, dout).astype(jnp.bfloat16)
    dqkv = jnp.concatenate([dq.reshape(frames, count, width), dk.reshape(frames, count, width), dv.reshape(frames, count, width)], axis=-1)
    return dqkv, attn.reshape(frames, count, width)


def reference(hidden_in, grad_out, w_qkv, w_out):
    frames, patches, width = hidden_in.shape
    rows_h = hidden_in.reshape(-1, width)
    rows_g = grad_out.reshape(-1, width)
    qkv = jnp.dot(rows_h, w_qkv, preferred_element_type=jnp.float32).astype(jnp.bfloat16)
    dout = jnp.dot(rows_g, w_out.T, preferred_element_type=jnp.float32).astype(jnp.bfloat16)
    blk = 8 if patches % 8 == 0 else 1
    nblk = patches // blk
    qkv_blocks = jnp.transpose(qkv.reshape(frames, nblk, blk, 3 * width), (1, 0, 2, 3))
    dout_blocks = jnp.transpose(dout.reshape(frames, nblk, blk, width), (1, 0, 2, 3))
    dqkv_blocks, attn_blocks = lax.map(attend_block, (qkv_blocks, dout_blocks))
    dqkv = jnp.transpose(dqkv_blocks, (1, 0, 2, 3)).reshape(-1, 3 * width)
    attn = jnp.transpose(attn_blocks, (1, 0, 2, 3)).reshape(-1, width)
    grad_wout = jnp.dot(attn.T, rows_g, preferred_element_type=jnp.float32)
    grad_in = jnp.dot(dqkv, w_qkv.T, preferred_element_type=jnp.float32).astype(jnp.bfloat16)
    grad_wqkv = jnp.dot(rows_h.T, dqkv, preferred_element_type=jnp.float32)
    return grad_in.reshape(frames, patches, width), grad_wqkv, grad_wout
```

```python
import jax
import jax.numpy as jnp
from jax import lax
from jax.sharding import Mesh, PartitionSpec as P

HEADS = 16
FRAME = ("x", "z", "yh")
Y = ("yh", "yl")
BF, F32 = jnp.bfloat16, jnp.float32


def flip(array, axes, step):
    size = 4 if axes == "x" or axes == Y else 2
    return lax.ppermute(array, axes, [(i, i ^ step) for i in range(size)])


def mm(a, b, contract):
    return lax.dot_general(a, b, (contract, ((), ())), preferred_element_type=F32)


def attend_rows(qkv, dout):
    patches, frames = 2, 128
    width = dout.shape[-1]
    head_size = width // HEADS
    scale = 1.0 / head_size**0.5
    shape = (patches, frames, HEADS, head_size)
    query, keys, values = (qkv[:, i * width : (i + 1) * width].reshape(shape) for i in range(3))
    dout = dout.reshape(shape)
    scores = jnp.einsum("pfhd,pghd->phfg", query, keys, preferred_element_type=F32) * scale
    probs = jax.nn.softmax(scores, axis=-1)
    probs_b = probs.astype(BF)
    attn = jnp.einsum("phfg,pghd->pfhd", probs_b, values, preferred_element_type=F32).astype(BF)
    dprob = jnp.einsum("pfhd,pghd->phfg", dout, values, preferred_element_type=F32)
    dscore = (probs * (dprob - jnp.sum(probs * dprob, axis=-1, keepdims=True)) * scale).astype(BF)
    grad_q = jnp.einsum("phfg,pghd->pfhd", dscore, keys, preferred_element_type=F32).astype(BF)
    grad_k = jnp.einsum("phfg,pfhd->pghd", dscore, query, preferred_element_type=F32).astype(BF)
    grad_v = jnp.einsum("phfg,pfhd->pghd", probs_b, dout, preferred_element_type=F32).astype(BF)
    rows = patches * frames
    dqkv = jnp.concatenate([g.reshape(rows, width) for g in (grad_q, grad_k, grad_v)], axis=-1)
    return dqkv, attn.reshape(rows, width)


def column_order(x, yh):
    at = jnp.arange(576)
    k, zz = at % 18, at // 18 % 4
    rx_a, ra_a = at // 144, at // 72 % 2
    ra_b, rx_b = at // 288, at // 72 % 4
    half_a = (x ^ rx_a) * 288 + zz * 36 + (yh ^ ra_a) * 18 + k
    half_b = (x ^ rx_b) * 288 + (4 + zz) * 36 + (yh ^ ra_b) * 18 + k
    return jnp.concatenate([half_a, half_b])


def per_device(hidden_in, grad_out, w_qkv, w_out):
    width = hidden_in.shape[-1]
    x, yh, yl, c = (lax.axis_index(a) for a in ("x", "yh", "yl", "c"))
    both = jnp.stack([hidden_in.reshape(2, 64, 2, width), grad_out.reshape(2, 64, 2, width)])
    both = both.transpose(2, 0, 1, 3, 4).reshape(512, width)
    both = lax.all_to_all(both, FRAME, split_axis=0, concat_axis=0, tiled=True)
    both = both.reshape(64, 2, 2, 2, width).transpose(1, 3, 0, 2, 4).reshape(2, 256, width)
    hid, gout = both[0], both[1]
    onehot = (jnp.arange(width)[:, None] == column_order(x, yh)[None, :]).astype(BF)
    hid_cols = mm(hid, onehot, ((1,), (0,))).astype(BF)
    gout_blocks = gout.reshape(256, 2, 2, 288)

    def block(arrays, rb, cc):
        part = lax.dynamic_index_in_dim(arrays, yl ^ rb, 1, keepdims=False)
        return lax.dynamic_index_in_dim(part, cc, 1, keepdims=False)

    def both_blocks(arrays, cc):
        return jnp.stack([block(arrays, 0, cc), block(arrays, 1, cc)])

    hid_other = flip(hid_cols, "c", 1)
    gout_other = flip(both_blocks(gout_blocks, 1 - c), "c", 1)
    qkv = mm(hid, w_qkv, ((1,), (0,))).astype(BF)
    dout = mm(gout, w_out, ((1,), (1,))).astype(BF)
    dqkv, attn = attend_rows(qkv, dout)
    attn_cols = mm(attn, onehot, ((1,), (0,))).astype(BF)
    dqkv_blocks = dqkv.reshape(256, 2, 2, 864)
    attn_other = flip(attn_cols, "c", 1)
    dqkv_other = flip(both_blocks(dqkv_blocks, 1 - c), "c", 1)
    hid2 = jnp.concatenate([hid_cols, hid_other])
    attn2 = jnp.concatenate([attn_cols, attn_other])
    dqkv2 = jnp.concatenate([both_blocks(dqkv_blocks, c), dqkv_other], axis=1)
    gout2 = jnp.concatenate([both_blocks(gout_blocks, c), gout_other], axis=1)

    def product(lo, hi):
        return jnp.stack(
            [
                jnp.concatenate(
                    [
                        mm(hid2[:, lo:hi], dqkv2[rb], ((0,), (0,))),
                        mm(attn2[:, lo:hi], gout2[rb], ((0,), (0,))),
                    ],
                    axis=1,
                ).astype(BF)
                for rb in range(2)
            ]
        )

    part_a = [product(144 * rx, 144 * (rx + 1)) for rx in range(4)]
    part_b = [product(576 + 288 * ra, 576 + 288 * (ra + 1)) for ra in range(2)]
    got_a = [flip(part_a[rx], "x", rx) for rx in (1, 3, 2)]
    got_b = [flip(part_b[s >> 1][s & 1], Y, s) for s in (1, 3, 2)]
    sum_a = part_a[0].astype(F32) + sum(g.astype(F32) for g in got_a)
    sum_b = part_b[0][0].astype(F32) + sum(g.astype(F32) for g in got_b)
    sum_a = sum_a.astype(BF).reshape(2, 2, 72, width)
    sum_b = sum_b.astype(BF).reshape(4, 72, width)
    got_a = [flip(sum_a[s & 1, s >> 1], Y, s) for s in (1, 3, 2)]
    got_b = [flip(sum_b[rx], "x", rx) for rx in (1, 3, 2)]
    sum_a = sum_a[0, 0].astype(F32) + sum(g.astype(F32) for g in got_a)
    sum_b = sum_b[0].astype(F32) + sum(g.astype(F32) for g in got_b)
    last = jnp.concatenate([sum_a, sum_b]).astype(BF).reshape(8, 18, width)
    last = lax.all_to_all(last, "z", split_axis=0, concat_axis=0, tiled=True)
    grad_w = jnp.sum(last.astype(F32), axis=0)

    grad_in = mm(dqkv, w_qkv, ((1,), (1,))).astype(BF)
    grad_in = grad_in.reshape(2, 64, 2, width).transpose(1, 2, 0, 3).reshape(256, width)
    grad_in = lax.all_to_all(grad_in, FRAME, split_axis=0, concat_axis=0, tiled=True)
    grad_in = grad_in.reshape(64, 2, 2, width).transpose(1, 0, 2, 3).reshape(2, 128, width)
    return grad_in, grad_w[:, :864], grad_w[:, 864:]


def solution(mesh):
    fine = Mesh(mesh.devices.reshape(4, 8, 2, 2, 2), ("x", "z", "yh", "yl", "c"))
    patch = ("yl", "c")
    in_specs = (P(FRAME, patch, None), P(FRAME, patch, None), P(), P())
    out_specs = (P(FRAME, patch, None), P(FRAME, patch), P(FRAME, patch))
    return jax.shard_map(
        per_device, mesh=fine, in_specs=in_specs, out_specs=out_specs, check_vma=False
    )
```

```python
import jax
import jax.numpy as jnp
from jax import lax
from jax.experimental import pallas as pl
from jax.experimental.pallas import tpu as pltpu
from jax.sharding import Mesh, PartitionSpec as P

HEADS, HD, D = 16, 72, 1152
ROWS = 256
FRAME = ("x", "z", "yh")
Y = ("yh", "yl")
BF, F32 = jnp.bfloat16, jnp.float32
NN = ((1,), (0,))
NT = ((1,), (1,))
TN = ((0,), (0,))
VMEM = pl.BlockSpec(memory_space=pltpu.VMEM)
ANY = pl.BlockSpec(memory_space=pl.ANY)
SMEM = pl.BlockSpec(memory_space=pltpu.SMEM)
LIMIT = 56 * 1024 * 1024


def flip(array, axes, step):
    size = 4 if axes == "x" or axes == Y else 2
    return lax.ppermute(array, axes, [(i, i ^ step) for i in range(size)])


def mm(a, b, contract):
    return lax.dot_general(a, b, (contract, ((), ())), preferred_element_type=F32)


def pick(rows, cols, source):
    i = lax.broadcasted_iota(jnp.int32, (rows, cols), 0)
    j = lax.broadcasted_iota(jnp.int32, (rows, cols), 1)
    return (j == source(i)).astype(F32).astype(BF)


def pack_kernel(hidden, grad, out):
    at = lambda a: pick(
        512, ROWS, lambda i: jnp.where(((i >> 2) & 1) == a, ((i >> 1) & 1) * 128 + (i >> 3) * 2 + (i & 1), -1)
    )
    out[...] = (mm(at(0), hidden[...], NN) + mm(at(1), grad[...], NN)).astype(BF)


def attend_kernel(blocks, got, order, w_qkv, w_out, x_out, dg_own, dg_other, dq_out,
                  w1, w2, sems, qkv_t, do_t, dqkv_t, attn_t):
    loads = [pltpu.make_async_copy(w_out, w2, sems.at[0])] + [
        pltpu.make_async_copy(w_qkv.at[:, pl.ds(D * i, D)], w1.at[i], sems.at[1 + i]) for i in range(3)
    ]
    for load in loads:
        load.start()
    place = lambda a: lambda i: ((i >> 1) & 63) * 8 + a * 4 + (i & 1) * 2 + (i >> 7)
    recv = got[...]
    hid = mm(pick(ROWS, 512, place(0)), recv, NN).astype(BF)
    gout = mm(pick(ROWS, 512, place(1)), recv, NN).astype(BF)
    gout_t = gout.astype(F32).T.astype(BF)
    for b in range(4):
        rows = gout_t[288 * b : 288 * (b + 1)]

        @pl.when(blocks[b] < 2)
        def _():
            dg_own[blocks[b], 864:, :] = rows

        @pl.when(blocks[b] >= 2)
        def _():
            dg_other[blocks[b] - 2, 864:, :] = rows

    chosen = [
        (lax.broadcasted_iota(jnp.int32, (384, D), 1) == order[384 * i : 384 * (i + 1), :])
        .astype(F32)
        .astype(BF)
        for i in range(3)
    ]
    for i in range(3):
        x_out[384 * i : 384 * (i + 1), :] = mm(chosen[i], hid, NT).astype(BF)
    loads[0].wait()
    for i in range(3):
        do_t[384 * i : 384 * (i + 1), :] = mm(w2[384 * i : 384 * (i + 1), :], gout, NT).astype(BF).astype(F32)
    for i in range(3):
        loads[1 + i].wait()
        for j in range(3):
            part = mm(hid, w1[i, :, 384 * j : 384 * (j + 1)], NN).astype(BF).astype(F32)
            qkv_t[D * i + 384 * j : D * i + 384 * (j + 1), :] = part.T

    scale = 1.0 / HD**0.5

    def head(h, carry):
        at = lambda i: pl.ds(pl.multiple_of(D * i + HD * h, 8), HD)
        q_t, k_t, v_t = (qkv_t[at(i), :].astype(BF) for i in range(3))
        d_t = do_t[at(0), :].astype(BF)
        results = []
        for p in range(2):
            cut = slice(128 * p, 128 * (p + 1))
            q, k, v, do = q_t[:, cut], k_t[:, cut], v_t[:, cut], d_t[:, cut]
            scores = mm(k, q, TN) * scale
            grown = jnp.exp(scores - jnp.max(scores, axis=0, keepdims=True))
            probs = grown * (1.0 / jnp.sum(grown, axis=0, keepdims=True))
            probs_b = probs.astype(BF)
            dprob = mm(v, do, TN)
            dscore = probs * (dprob - jnp.sum(probs * dprob, axis=0, keepdims=True)) * scale
            dscore = dscore.astype(BF)
            attn_t[at(0), cut] = mm(v, probs_b, NN)
            dqkv_t[at(0), cut] = mm(k, dscore, NN)
            dqkv_t[at(1), cut] = mm(q, dscore, NT)
            dqkv_t[at(2), cut] = mm(do, probs_b, NT)
        return carry

    lax.fori_loop(0, HEADS, head, 0, unroll=4)

    attn = attn_t[...].astype(BF)
    for i in range(3):
        x_out[D + 384 * i : D + 384 * (i + 1), :] = mm(chosen[i], attn, NN).astype(BF)
    back = pick(ROWS, ROWS, lambda i: (i & 127) * 2 + (i >> 7))
    for b in range(4):
        rows = dqkv_t[864 * b : 864 * (b + 1), :].astype(BF)

        @pl.when(blocks[b] < 2)
        def _():
            dg_own[blocks[b], :864, :] = rows

        @pl.when(blocks[b] >= 2)
        def _():
            dg_other[blocks[b] - 2, :864, :] = rows

        dq_out[864 * b : 864 * (b + 1), :] = mm(rows, back, NN).astype(BF)


def product_kernel(x_own, x_oth, dg_own, dg_oth, *parts):
    row = lax.broadcasted_iota(jnp.int32, (128, ROWS), 0)
    for r in range(2):
        for s in range(8):
            rows = 144
            cut = slice(rows * s, rows * (s + 1))
            low = slice(D + rows * s, D + rows * (s + 1))
            pieces = []
            for lo in (0, 384):
                pieces.append(mm(x_own[cut, :], dg_own[r, lo : lo + 384, :], NT)
                              + mm(x_oth[cut, :], dg_oth[r, lo : lo + 384, :], NT))
            own, oth = dg_own[r, 768:896, :], dg_oth[r, 768:896, :]
            none = jnp.zeros_like(own)
            mixed = (mm(x_own[cut, :], jnp.where(row < 96, own, none), NT)
                     + mm(x_oth[cut, :], jnp.where(row < 96, oth, none), NT)
                     + mm(x_own[low, :], jnp.where(row >= 96, own, none), NT)
                     + mm(x_oth[low, :], jnp.where(row >= 96, oth, none), NT))
            right = (mm(x_own[low, :], dg_own[r, 896:, :], NT)
                     + mm(x_oth[low, :], dg_oth[r, 896:, :], NT))
            if s < 4:
                out, at = parts[s], slice(None)
                put = lambda c, v: out.__setitem__((r, at, c), v.astype(BF))
            else:
                ra, half = (s - 4) // 2, (s - 4) % 2
                out, at = parts[4 + 2 * ra + r], slice(rows * half, rows * (half + 1))
                put = lambda c, v: out.__setitem__((at, c), v.astype(BF))
            put(slice(0, 384), pieces[0])
            put(slice(384, 768), pieces[1])
            put(slice(768, 896), mixed)
            put(slice(896, D), right)


def shape(*dims, dtype=BF):
    return jax.ShapeDtypeStruct(dims, dtype)


def call(kernel, outs, ins, flops, scratch=(), specs=None):
    return pl.pallas_call(
        kernel,
        out_shape=outs,
        in_specs=specs or [VMEM] * len(ins),
        out_specs=jax.tree.map(lambda _: VMEM, outs),
        scratch_shapes=list(scratch),
        compiler_params=pltpu.CompilerParams(vmem_limit_bytes=LIMIT),
        cost_estimate=pl.CostEstimate(flops=flops, bytes_accessed=10**7, transcendentals=0),
    )(*ins)


def column_order(x, yh):
    at = jnp.arange(576)
    k, zz = at % 18, at // 18 % 4
    rx_a, ra_a = at // 144, at // 72 % 2
    ra_b, rx_b = at // 288, at // 72 % 4
    half_a = (x ^ rx_a) * 288 + zz * 36 + (yh ^ ra_a) * 18 + k
    half_b = (x ^ rx_b) * 288 + (4 + zz) * 36 + (yh ^ ra_b) * 18 + k
    return jnp.concatenate([half_a, half_b])


def total(own, others):
    return own.astype(F32) + sum(g.astype(F32) for g in others)


def per_device(hidden_in, grad_out, w_qkv, w_out):
    x, yh, yl, c = (lax.axis_index(a) for a in ("x", "yh", "yl", "c"))
    both = call(pack_kernel, shape(512, D), (hidden_in.reshape(ROWS, D), grad_out.reshape(ROWS, D)), 10**9)
    both = lax.all_to_all(both, FRAME, split_axis=0, concat_axis=0, tiled=True)
    order = column_order(x, yh).astype(jnp.int32).reshape(D, 1)
    blocks = jnp.stack([(b // 2 ^ yl) + 2 * (b % 2 ^ c) for b in range(4)]).astype(jnp.int32)
    x_own, dg_own, dg_other, dqkv = call(
        attend_kernel,
        (shape(2 * D, ROWS), shape(2, D, ROWS), shape(2, D, ROWS), shape(3 * D, ROWS)),
        (blocks, both, order, w_qkv, w_out),
        10 * 10**9,
        scratch=[
            pltpu.VMEM((3, D, D), BF),
            pltpu.VMEM((D, D), BF),
            pltpu.SemaphoreType.DMA((4,)),
            pltpu.VMEM((3 * D, ROWS), F32),
            pltpu.VMEM((D, ROWS), F32),
            pltpu.VMEM((3 * D, ROWS), F32),
            pltpu.VMEM((D, ROWS), F32),
        ],
        specs=[SMEM, VMEM, VMEM, ANY, ANY],
    )
    x_oth, dg_oth = flip(x_own, "c", 1), flip(dg_other, "c", 1)
    parts = call(
        product_kernel,
        [shape(2, 144, D)] * 4 + [shape(288, D)] * 4,
        (x_own, x_oth, dg_own, dg_oth),
        6 * 10**9,
    )
    part_a, part_b = parts[:4], parts[4:]
    got_a = [flip(part_a[rx], "x", rx) for rx in (1, 3, 2)]
    got_b = [flip(part_b[s], Y, s) for s in (1, 3, 2)]
    sum_a = total(part_a[0], got_a).astype(BF).reshape(2, 2, 72, D)
    sum_b = total(part_b[0], got_b).astype(BF).reshape(4, 72, D)
    got_a = [flip(sum_a[s & 1, s >> 1], Y, s) for s in (1, 3, 2)]
    got_b = [flip(sum_b[rx], "x", rx) for rx in (1, 3, 2)]
    last = jnp.concatenate([total(sum_a[0, 0], got_a), total(sum_b[0], got_b)])
    last = last.astype(BF).reshape(8, 18, D)
    last = lax.all_to_all(last, "z", split_axis=0, concat_axis=0, tiled=True)
    grad_w = jnp.sum(last.astype(F32), axis=0)

    grad_in = mm(dqkv, w_qkv, ((0,), (1,))).astype(BF)
    grad_in = lax.all_to_all(grad_in, FRAME, split_axis=0, concat_axis=0, tiled=True)
    grad_in = grad_in.reshape(64, 2, 2, D).transpose(1, 0, 2, 3).reshape(2, 128, D)
    return grad_in, grad_w[:, :864], grad_w[:, 864:]


def solution(mesh):
    fine = Mesh(mesh.devices.reshape(4, 8, 2, 2, 2), ("x", "z", "yh", "yl", "c"))
    patch = ("yl", "c")
    in_specs = (P(FRAME, patch, None), P(FRAME, patch, None), P(), P())
    out_specs = (P(FRAME, patch, None), P(FRAME, patch), P(FRAME, patch))
    return jax.shard_map(
        per_device, mesh=fine, in_specs=in_specs, out_specs=out_specs, check_vma=False
    )
```

```python
import jax
import jax.numpy as jnp
from jax import lax
from jax.experimental import pallas as pl
from jax.experimental.pallas import tpu as pltpu
from jax.sharding import Mesh, PartitionSpec as P

HEADS, HD, D = 16, 72, 1152
ROWS = 256
FRAME = ("x", "z", "yh")
Y = ("yh", "yl")
BF, F32 = jnp.bfloat16, jnp.float32
NN = ((1,), (0,))
NT = ((1,), (1,))
TN = ((0,), (0,))
VMEM = pl.BlockSpec(memory_space=pltpu.VMEM)
ANY = pl.BlockSpec(memory_space=pl.ANY)
SMEM = pl.BlockSpec(memory_space=pltpu.SMEM)
MIB = 1024 * 1024
CUTS = 2


def flip(array, axes, step):
    size = {"x": 4, "z": 8, Y: 4, "c": 2}[axes]
    return lax.ppermute(array, axes, [(i, i ^ step) for i in range(size)])


def mm(a, b, contract):
    return lax.dot_general(a, b, (contract, ((), ())), preferred_element_type=F32)


def pick(rows, cols, source):
    i = lax.broadcasted_iota(jnp.int32, (rows, cols), 0)
    j = lax.broadcasted_iota(jnp.int32, (rows, cols), 1)
    return (j == source(i)).astype(F32).astype(BF)


def pack_kernel(hidden, grad, out, held, sent, sems):
    loads = [pltpu.make_async_copy(array, held.at[i], sems.at[i]) for i, array in enumerate((hidden, grad))]
    for load in loads:
        load.start()
    at = lambda a: pick(
        512, ROWS, lambda i: jnp.where(((i >> 2) & 1) == a, ((i >> 1) & 1) * 128 + (i >> 3) * 2 + (i & 1), -1)
    )
    for load in loads:
        load.wait()
    sent[...] = (mm(at(0), held[0], NN) + mm(at(1), held[1], NN)).astype(BF)
    store = pltpu.make_async_copy(sent, out, sems.at[2])
    store.start()
    store.wait()


def column_order(place, start, count):
    x, z, yh = place[0], place[1], place[2]
    at = lax.broadcasted_iota(jnp.int32, (count, 1), 0) + start
    q = ((at.astype(F32) + 0.5) * (1.0 / 18)).astype(jnp.int32)
    first = q < 32
    rx = jnp.where(first, q >> 3, (q >> 2) & 3)
    ra = jnp.where(first, (q >> 2) & 1, (q >> 4) & 1)
    rz = (q & 3) + jnp.where(first, 0, 4)
    return (x ^ rx) * 288 + (z ^ rz) * 36 + (yh ^ ra) * 18 + (at - 18 * q)


def slot(place, b):
    return ((b // 2) ^ place[3]) + 2 * ((b % 2) ^ place[4])


def prepare_kernel(place, w_qkv, w_out, out, held, made, sems):
    loads = [
        pltpu.make_async_copy(w_qkv.at[:, pl.ds(D * i, D)], held.at[i], sems.at[i]) for i in range(3)
    ] + [pltpu.make_async_copy(w_out, made.at[pl.ds(3 * D, D)], sems.at[3])]
    for load in loads:
        load.start()
    for i in range(3):
        order = column_order(place, 384 * i, 384)
        cols = lax.broadcasted_iota(jnp.int32, (384, D), 1)
        made[4 * D + 384 * i : 4 * D + 384 * (i + 1), :] = (cols == order).astype(F32).astype(BF)
    for i in range(3):
        loads[i].wait()
        for j in range(3):
            made[D * i + 384 * j : D * i + 384 * (j + 1), :] = held[i, :, 384 * j : 384 * (j + 1)].T
    loads[3].wait()
    store = pltpu.make_async_copy(made, out.at[pl.ds(0, 5 * D)], sems.at[4])
    store.start()
    store.wait()


def attend_kernel(home, got, prepared, x_out, dg_own, dg_other, weights, sems, qkv_t, do_t, dqkv_t, attn_t):
    order = (3, 0, 1, 2, 4)
    loads = [pltpu.make_async_copy(prepared.at[pl.ds(D * i, D)], weights.at[i], sems.at[i]) for i in order]
    for load in loads:
        load.start()
    place = lambda a: lambda i: ((i >> 1) & 63) * 8 + a * 4 + (i & 1) * 2 + (i >> 7)
    gout = mm(pick(ROWS, 512, place(1)), got[...], NN).astype(BF)
    hid = mm(pick(ROWS, 512, place(0)), got[...], NN).astype(BF)
    loads[0].wait()
    for i in range(3):
        cut = slice(384 * i, 384 * (i + 1))
        do_t[cut, :] = mm(weights[3, cut, :], gout, NT).astype(BF).astype(F32)
    for i in range(3):
        loads[1 + i].wait()
        for j in range(3):
            part = mm(weights[i, 384 * j : 384 * (j + 1), :], hid, NT)
            qkv_t[D * i + 384 * j : D * i + 384 * (j + 1), :] = part.astype(BF).astype(F32)

    def keep(b, rows, at):
        @pl.when(slot(home, b) < 2)
        def _():
            dg_own[slot(home, b) & 1, at, :] = rows

        @pl.when(slot(home, b) >= 2)
        def _():
            dg_other[slot(home, b) & 1, at, :] = rows

    gout_t = gout.T
    for b in range(4):
        keep(b, gout_t[288 * b : 288 * (b + 1)], slice(864, D))

    scale = 1.0 / HD**0.5

    def head(h, carry):
        at = lambda i: pl.ds(pl.multiple_of(D * i + HD * h, 8), HD)
        q_t, k_t, v_t = (qkv_t[at(i), :].astype(BF) for i in range(3))
        d_t = do_t[at(0), :].astype(BF)
        for p in range(2):
            cut = slice(128 * p, 128 * (p + 1))
            q, k, v, do = q_t[:, cut], k_t[:, cut], v_t[:, cut], d_t[:, cut]
            scores = mm(k, q, TN) * scale
            grown = jnp.exp(scores - jnp.max(scores, axis=0, keepdims=True))
            probs = grown * (1.0 / jnp.sum(grown, axis=0, keepdims=True))
            probs_b = probs.astype(BF)
            dprob = mm(v, do, TN)
            dscore = probs * (dprob - jnp.sum(probs * dprob, axis=0, keepdims=True)) * scale
            dscore = dscore.astype(BF)
            attn_t[at(0), cut] = mm(v, probs_b, NN)
            dqkv_t[at(0), cut] = mm(k, dscore, NN)
            dqkv_t[at(1), cut] = mm(q, dscore, NT)
            dqkv_t[at(2), cut] = mm(do, probs_b, NT)
        return carry

    lax.fori_loop(0, HEADS, head, 0, unroll=16)

    attn = attn_t[...].astype(BF)
    loads[4].wait()
    for i in range(3):
        chosen = weights[4, 384 * i : 384 * (i + 1), :]
        x_out[384 * i : 384 * (i + 1), :] = mm(chosen, hid, NT).astype(BF)
        x_out[D + 384 * i : D + 384 * (i + 1), :] = mm(chosen, attn, NN).astype(BF)
    for b in range(4):
        keep(b, dqkv_t[864 * b : 864 * (b + 1), :].astype(BF), slice(0, 864))


def grad_in_kernel(home, dg_own, dg_other, prepared, out, w_t, sent, sems):
    loads = [pltpu.make_async_copy(prepared.at[pl.ds(864 * i, 864)], w_t.at[i], sems.at[i]) for i in range(4)]
    for load in loads:
        load.start()
    total = None
    for b in range(4):
        kept = dg_own[slot(home, b) & 1, :864, :]
        away = dg_other[slot(home, b) & 1, :864, :]
        rows = jnp.where(slot(home, b) < 2, kept, away)
        loads[b].wait()
        part = mm(rows, w_t[b], TN)
        total = part if total is None else total + part
    total = total.astype(BF)
    at = lambda a: pick(
        512, ROWS, lambda i: jnp.where(((i >> 2) & 1) == a, (i & 1) * 128 + (i >> 3) * 2 + ((i >> 1) & 1), -1)
    )
    sent[...] = (mm(at(0), total[:, :640], NN) + mm(at(1), total[:, 512:], NN)).astype(BF)
    store = pltpu.make_async_copy(sent, out, sems.at[4])
    store.start()
    store.wait()


def unpack_kernel(got, out):
    recv = got[...]
    at = lambda a: pick(ROWS, 512, lambda i: ((i >> 1) & 63) * 8 + a * 4 + (i >> 7) * 2 + (i & 1))
    out[:, :640] = mm(at(0), recv, NN).astype(BF)
    out[:, 640:] = mm(at(1), recv[:, 128:], NN).astype(BF)


def product_kernel(x_own, x_oth, dg_own, dg_oth, *parts):
    row = lax.broadcasted_iota(jnp.int32, (128, 2 * ROWS), 0)
    both = lambda at: jnp.concatenate([x_own[at, :], x_oth[at, :]], axis=1)
    for r in range(2):
        d_all = jnp.concatenate([dg_own[r], dg_oth[r]], axis=1)
        edge = d_all[768:896]
        none = jnp.zeros_like(edge)
        edge = jnp.concatenate([jnp.where(row < 96, edge, none), jnp.where(row < 96, none, edge)], axis=1)
        for s in range(0, 8, 8 // CUTS):
            rows = D // CUTS
            hid = both(slice(144 * s, 144 * s + rows))
            attn = both(slice(D + 144 * s, D + 144 * s + rows))
            pieces = [
                (0, mm(hid, d_all[:384], NT)),
                (384, mm(hid, d_all[384:768], NT)),
                (768, mm(jnp.concatenate([hid, attn], axis=1), edge, NT)),
                (896, mm(attn, d_all[896:], NT)),
            ]
            for lo, piece in pieces:
                cols = slice(lo, lo + piece.shape[1])
                piece = piece.astype(BF)
                for t in range(8 // CUTS):
                    part = piece[144 * t : 144 * (t + 1)]
                    if s + t < 4:
                        parts[s + t][r, :, cols] = part
                    else:
                        ra, half = divmod(s + t - 4, 2)
                        parts[4 + 2 * ra + r][144 * half : 144 * (half + 1), cols] = part


def shape(*dims, dtype=BF):
    return jax.ShapeDtypeStruct(dims, dtype)


def call(kernel, outs, ins, flops, mib, scratch=(), specs=None):
    return pl.pallas_call(
        kernel,
        out_shape=outs,
        in_specs=specs or [VMEM] * len(ins),
        out_specs=[VMEM] * len(outs) if isinstance(outs, list) else ANY,
        scratch_shapes=list(scratch),
        compiler_params=pltpu.CompilerParams(vmem_limit_bytes=mib * MIB),
        cost_estimate=pl.CostEstimate(flops=flops, bytes_accessed=10**7, transcendentals=0),
    )(*ins)


def prepare_call(place, w_qkv, w_out):
    return call(
        prepare_kernel,
        shape(14 * D, D),
        (place, w_qkv, w_out),
        10**9,
        32,
        scratch=[pltpu.VMEM((3, D, D), BF), pltpu.VMEM((5 * D, D), BF), pltpu.SemaphoreType.DMA((5,))],
        specs=[SMEM, ANY, ANY],
    )


def attend_call(place, both, prepared):
    return call(
        attend_kernel,
        [shape(2 * D, ROWS), shape(2, D, ROWS), shape(2, D, ROWS)],
        (place, both, prepared),
        10 * 10**9,
        28,
        scratch=[
            pltpu.VMEM((5, D, D), BF),
            pltpu.SemaphoreType.DMA((5,)),
            pltpu.VMEM((3 * D, ROWS), F32),
            pltpu.VMEM((D, ROWS), F32),
            pltpu.VMEM((3 * D, ROWS), F32),
            pltpu.VMEM((D, ROWS), F32),
        ],
        specs=[SMEM, VMEM, ANY],
    )


def total(own, others):
    return own.astype(F32) + sum(g.astype(F32) for g in others)


def per_device(hidden_in, grad_out, w_qkv, w_out):
    place = jnp.stack([lax.axis_index(a) for a in ("x", "z", "yh", "yl", "c")]).astype(jnp.int32)
    both = call(
        pack_kernel,
        shape(512, D),
        (hidden_in.reshape(ROWS, D), grad_out.reshape(ROWS, D)),
        10**9,
        58,
        scratch=[pltpu.VMEM((2, ROWS, D), BF), pltpu.VMEM((512, D), BF), pltpu.SemaphoreType.DMA((3,))],
        specs=[ANY, ANY],
    )
    both = lax.all_to_all(both, FRAME, split_axis=0, concat_axis=0, tiled=True)
    prepared = prepare_call(place, w_qkv, w_out)
    x_own, dg_own, dg_other = attend_call(place, both, prepared)
    x_oth, dg_oth = flip(x_own, "c", 1), flip(dg_other, "c", 1)
    parts = call(
        product_kernel,
        [shape(2, 144, D)] * 4 + [shape(288, D)] * 4,
        (x_own, x_oth, dg_own, dg_oth),
        6 * 10**9,
        20,
    )
    part_a, part_b = parts[:4], parts[4:]
    got_a, got_b = [], []
    for s in (2, 1, 3):
        got_a.append(flip(part_a[s], "x", s))
        got_b.append(flip(part_b[s], Y, s))

    dg_own, dg_other, _ = lax.optimization_barrier((dg_own, dg_other, got_a[0]))
    grad_in = call(
        grad_in_kernel,
        shape(512, 640),
        (place, dg_own, dg_other, prepared),
        3 * 10**9,
        20,
        scratch=[pltpu.VMEM((4, 864, D), BF), pltpu.VMEM((512, 640), BF), pltpu.SemaphoreType.DMA((5,))],
        specs=[SMEM, VMEM, VMEM, ANY],
    )

    sum_a = total(part_a[0], got_a).astype(BF).reshape(2, 2, 72, D)
    sum_b = total(part_b[0], got_b).astype(BF).reshape(4, 72, D)
    got_a, got_b = [], []
    for s in (2, 1, 3):
        got_a.append(flip(sum_a[s & 1, s >> 1], Y, s))
        got_b.append(flip(sum_b[s], "x", s))
    sum_a = total(sum_a[0, 0], got_a).reshape(4, 18, D)
    sum_b = total(sum_b[0], got_b).reshape(4, 18, D)
    got = [flip(jnp.concatenate([sum_a[s], sum_b[s]]).astype(BF), "z", s) for s in (2, 1, 3)]
    near = total(sum_a[0], [g[:18] for g in got])
    far = flip(total(sum_b[0], [g[18:] for g in got]).astype(BF), "z", 4)
    grad_wqkv = total(near[:, :864], [far[:, :864]])
    grad_wout = total(near[:, 864:], [far[:, 864:]])
    grad_in = lax.all_to_all(grad_in, FRAME, split_axis=0, concat_axis=0, tiled=True)
    (grad_in,) = call(unpack_kernel, [shape(ROWS, D)], (grad_in,), 10**9, 16)
    return grad_in.reshape(2, 128, D), grad_wqkv, grad_wout


def solution(mesh):
    fine = Mesh(mesh.devices.reshape(4, 8, 2, 2, 2), ("x", "z", "yh", "yl", "c"))
    patch = ("yl", "c")
    in_specs = (P(FRAME, patch, None), P(FRAME, patch, None), P(), P())
    out_specs = (P(FRAME, patch, None), P(FRAME, patch), P(FRAME, patch))
    return jax.shard_map(
        per_device, mesh=fine, in_specs=in_specs, out_specs=out_specs, check_vma=False
    )
```

```python
import jax
import jax.numpy as jnp
from jax import lax
from jax.experimental import pallas as pl
from jax.experimental.pallas import tpu as pltpu
from jax.sharding import Mesh, PartitionSpec as P

HEADS, HD, D = 16, 72, 1152
ROWS = 256
FRAME = ("x", "z", "yh")
Y = ("yh", "yl")
BF, F32 = jnp.bfloat16, jnp.float32
NN = ((1,), (0,))
NT = ((1,), (1,))
TN = ((0,), (0,))
VMEM = pl.BlockSpec(memory_space=pltpu.VMEM)
ANY = pl.BlockSpec(memory_space=pl.ANY)
SMEM = pl.BlockSpec(memory_space=pltpu.SMEM)
MIB = 1024 * 1024
CUTS = 2
TOGETHER = 4


def flip(array, axes, step):
    size = {"x": 4, "z": 8, Y: 4, "c": 2}[axes]
    return lax.ppermute(array, axes, [(i, i ^ step) for i in range(size)])


def mm(a, b, contract):
    return lax.dot_general(a, b, (contract, ((), ())), preferred_element_type=F32)


def pick(rows, cols, source):
    i = lax.broadcasted_iota(jnp.int32, (rows, cols), 0)
    j = lax.broadcasted_iota(jnp.int32, (rows, cols), 1)
    return (j == source(i)).astype(F32).astype(BF)


def pack_kernel(hidden, grad, out, held, sent, sems):
    loads = [pltpu.make_async_copy(array, held.at[i], sems.at[i]) for i, array in enumerate((hidden, grad))]
    for load in loads:
        load.start()
    at = lambda a: pick(
        512, ROWS, lambda i: jnp.where(((i >> 2) & 1) == a, ((i >> 1) & 1) * 128 + (i >> 3) * 2 + (i & 1), -1)
    )
    for load in loads:
        load.wait()
    sent[...] = (mm(at(0), held[0], NN) + mm(at(1), held[1], NN)).astype(BF)
    store = pltpu.make_async_copy(sent, out, sems.at[2])
    store.start()
    store.wait()


def column_order(place, start, count):
    x, z, yh = place[0], place[1], place[2]
    at = lax.broadcasted_iota(jnp.int32, (count, 1), 0) + start
    q = ((at.astype(F32) + 0.5) * (1.0 / 18)).astype(jnp.int32)
    first = q < 32
    rx = jnp.where(first, q >> 3, (q >> 2) & 3)
    ra = jnp.where(first, (q >> 2) & 1, (q >> 4) & 1)
    rz = ((q & 1) + 3 * (q & 2)) ^ jnp.where(first, 0, 2)
    return (x ^ rx) * 288 + (z ^ rz) * 36 + (yh ^ ra) * 18 + (at - 18 * q)


def slot(place, b):
    return ((b // 2) ^ place[3]) + 2 * ((b % 2) ^ place[4])


def prepare_kernel(place, w_qkv, w_out, out, held, made, sems):
    loads = [
        pltpu.make_async_copy(w_qkv.at[:, pl.ds(D * i, D)], held.at[i], sems.at[i]) for i in range(3)
    ] + [pltpu.make_async_copy(w_out, made.at[pl.ds(3 * D, D)], sems.at[3])]
    for load in loads:
        load.start()
    for i in range(3):
        order = column_order(place, 384 * i, 384)
        cols = lax.broadcasted_iota(jnp.int32, (384, D), 1)
        made[4 * D + 384 * i : 4 * D + 384 * (i + 1), :] = (cols == order).astype(F32).astype(BF)
    for i in range(3):
        loads[i].wait()
        for j in range(3):
            made[D * i + 384 * j : D * i + 384 * (j + 1), :] = held[i, :, 384 * j : 384 * (j + 1)].T
    loads[3].wait()
    store = pltpu.make_async_copy(made, out.at[pl.ds(0, 5 * D)], sems.at[4])
    store.start()
    store.wait()


def attend_kernel(home, got, prepared, x_out, dg_own, dg_other, weights, sems, qkv_t, do_t, dqkv_t, attn_t):
    order = (3, 0, 1, 2, 4)
    loads = [pltpu.make_async_copy(prepared.at[pl.ds(D * i, D)], weights.at[i], sems.at[i]) for i in order]
    for load in loads:
        load.start()
    place = lambda a: lambda i: ((i >> 1) & 63) * 8 + a * 4 + (i & 1) * 2 + (i >> 7)
    gout = mm(pick(ROWS, 512, place(1)), got[...], NN).astype(BF)
    hid = mm(pick(ROWS, 512, place(0)), got[...], NN).astype(BF)
    loads[0].wait()
    for i in range(3):
        cut = slice(384 * i, 384 * (i + 1))
        do_t[cut, :] = mm(weights[3, cut, :], gout, NT).astype(BF).astype(F32)
    for i in range(3):
        loads[1 + i].wait()
        for j in range(3):
            part = mm(weights[i, 384 * j : 384 * (j + 1), :], hid, NT)
            qkv_t[D * i + 384 * j : D * i + 384 * (j + 1), :] = part.astype(BF).astype(F32)

    def keep(b, rows, at):
        @pl.when(slot(home, b) < 2)
        def _():
            dg_own[slot(home, b) & 1, at, :] = rows

        @pl.when(slot(home, b) >= 2)
        def _():
            dg_other[slot(home, b) & 1, at, :] = rows

    gout_t = gout.T
    for b in range(4):
        keep(b, gout_t[288 * b : 288 * (b + 1)], slice(864, D))

    scale = 1.0 / HD**0.5

    def heads(t, carry):
        at = lambda i, h: pl.ds(pl.multiple_of(D * i + HD * (t * TOGETHER + h), 8), HD)
        pairs = []
        for h in range(TOGETHER):
            q_t, k_t, v_t = (qkv_t[at(i, h), :].astype(BF) for i in range(3))
            d_t = do_t[at(0, h), :].astype(BF)
            for p in range(2):
                cut = slice(128 * p, 128 * (p + 1))
                pairs.append((h, cut, q_t[:, cut], k_t[:, cut], v_t[:, cut], d_t[:, cut]))
        scores = [mm(k, q, TN) * scale for h, cut, q, k, v, do in pairs]
        dprobs = [mm(v, do, TN) for h, cut, q, k, v, do in pairs]
        probs = []
        for s in scores:
            grown = jnp.exp(s - jnp.max(s, axis=0, keepdims=True))
            probs.append(grown * (1.0 / jnp.sum(grown, axis=0, keepdims=True)))
        probs_b = [p.astype(BF) for p in probs]
        dscores = [(p * (d - jnp.sum(p * d, axis=0, keepdims=True)) * scale).astype(BF) for p, d in zip(probs, dprobs)]
        for (h, cut, q, k, v, do), p in zip(pairs, probs_b):
            attn_t[at(0, h), cut] = mm(v, p, NN)
            dqkv_t[at(2, h), cut] = mm(do, p, NT)
        for (h, cut, q, k, v, do), d in zip(pairs, dscores):
            dqkv_t[at(0, h), cut] = mm(k, d, NN)
            dqkv_t[at(1, h), cut] = mm(q, d, NT)
        return carry

    lax.fori_loop(0, HEADS // TOGETHER, heads, 0, unroll=4)

    attn = attn_t[...].astype(BF)
    loads[4].wait()
    for i in range(3):
        chosen = weights[4, 384 * i : 384 * (i + 1), :]
        x_out[384 * i : 384 * (i + 1), :] = mm(chosen, hid, NT).astype(BF)
        x_out[D + 384 * i : D + 384 * (i + 1), :] = mm(chosen, attn, NN).astype(BF)
    for b in range(4):
        keep(b, dqkv_t[864 * b : 864 * (b + 1), :].astype(BF), slice(0, 864))


def grad_in_kernel(home, dg_own, dg_other, prepared, out, w_t, sent, sems):
    loads = [pltpu.make_async_copy(prepared.at[pl.ds(864 * i, 864)], w_t.at[i], sems.at[i]) for i in range(4)]
    for load in loads:
        load.start()
    total = None
    for b in range(4):
        kept = dg_own[slot(home, b) & 1, :864, :]
        away = dg_other[slot(home, b) & 1, :864, :]
        rows = jnp.where(slot(home, b) < 2, kept, away)
        loads[b].wait()
        part = mm(rows, w_t[b], TN)
        total = part if total is None else total + part
    total = total.astype(BF)
    at = lambda a: pick(
        512, ROWS, lambda i: jnp.where(((i >> 2) & 1) == a, (i & 1) * 128 + (i >> 3) * 2 + ((i >> 1) & 1), -1)
    )
    sent[...] = (mm(at(0), total[:, :640], NN) + mm(at(1), total[:, 512:], NN)).astype(BF)
    store = pltpu.make_async_copy(sent, out, sems.at[4])
    store.start()
    store.wait()


def unpack_kernel(got, out):
    recv = got[...]
    at = lambda a: pick(ROWS, 512, lambda i: ((i >> 1) & 63) * 8 + a * 4 + (i >> 7) * 2 + (i & 1))
    out[:, :640] = mm(at(0), recv, NN).astype(BF)
    out[:, 640:] = mm(at(1), recv[:, 128:], NN).astype(BF)


def product_kernel(x_own, x_oth, dg_own, dg_oth, *parts):
    row = lax.broadcasted_iota(jnp.int32, (128, 2 * ROWS), 0)
    both = lambda at: jnp.concatenate([x_own[at, :], x_oth[at, :]], axis=1)
    for r in range(2):
        d_all = jnp.concatenate([dg_own[r], dg_oth[r]], axis=1)
        edge = d_all[768:896]
        none = jnp.zeros_like(edge)
        edge = jnp.concatenate([jnp.where(row < 96, edge, none), jnp.where(row < 96, none, edge)], axis=1)
        for s in range(0, 8, 8 // CUTS):
            rows = D // CUTS
            hid = both(slice(144 * s, 144 * s + rows))
            attn = both(slice(D + 144 * s, D + 144 * s + rows))
            pieces = [
                (0, mm(hid, d_all[:384], NT)),
                (384, mm(hid, d_all[384:768], NT)),
                (768, mm(jnp.concatenate([hid, attn], axis=1), edge, NT)),
                (896, mm(attn, d_all[896:], NT)),
            ]
            for lo, piece in pieces:
                cols = slice(lo, lo + piece.shape[1])
                piece = piece.astype(BF)
                for t in range(8 // CUTS):
                    part = piece[144 * t : 144 * (t + 1)]
                    if s + t < 4:
                        parts[s + t][r, :, cols] = part
                    else:
                        ra, half = divmod(s + t - 4, 2)
                        parts[4 + 2 * ra + r][144 * half : 144 * (half + 1), cols] = part


def shape(*dims, dtype=BF):
    return jax.ShapeDtypeStruct(dims, dtype)


def call(kernel, outs, ins, flops, mib, scratch=(), specs=None):
    return pl.pallas_call(
        kernel,
        out_shape=outs,
        in_specs=specs or [VMEM] * len(ins),
        out_specs=[VMEM] * len(outs) if isinstance(outs, list) else ANY,
        scratch_shapes=list(scratch),
        compiler_params=pltpu.CompilerParams(vmem_limit_bytes=mib * MIB),
        cost_estimate=pl.CostEstimate(flops=flops, bytes_accessed=10**7, transcendentals=0),
    )(*ins)


def prepare_call(place, w_qkv, w_out):
    return call(
        prepare_kernel,
        shape(14 * D, D),
        (place, w_qkv, w_out),
        10**9,
        32,
        scratch=[pltpu.VMEM((3, D, D), BF), pltpu.VMEM((5 * D, D), BF), pltpu.SemaphoreType.DMA((5,))],
        specs=[SMEM, ANY, ANY],
    )


def attend_call(place, both, prepared):
    return call(
        attend_kernel,
        [shape(2 * D, ROWS), shape(2, D, ROWS), shape(2, D, ROWS)],
        (place, both, prepared),
        10 * 10**9,
        28,
        scratch=[
            pltpu.VMEM((5, D, D), BF),
            pltpu.SemaphoreType.DMA((5,)),
            pltpu.VMEM((3 * D, ROWS), F32),
            pltpu.VMEM((D, ROWS), F32),
            pltpu.VMEM((3 * D, ROWS), F32),
            pltpu.VMEM((D, ROWS), F32),
        ],
        specs=[SMEM, VMEM, ANY],
    )


def total(own, others):
    return own.astype(F32) + sum(g.astype(F32) for g in others)


def per_device(hidden_in, grad_out, w_qkv, w_out):
    place = jnp.stack([lax.axis_index(a) for a in ("x", "z", "yh", "yl", "c")]).astype(jnp.int32)
    both = call(
        pack_kernel,
        shape(512, D),
        (hidden_in.reshape(ROWS, D), grad_out.reshape(ROWS, D)),
        10**9,
        58,
        scratch=[pltpu.VMEM((2, ROWS, D), BF), pltpu.VMEM((512, D), BF), pltpu.SemaphoreType.DMA((3,))],
        specs=[ANY, ANY],
    )
    both = lax.all_to_all(both, FRAME, split_axis=0, concat_axis=0, tiled=True)
    prepared = prepare_call(place, w_qkv, w_out)
    x_own, dg_own, dg_other = attend_call(place, both, prepared)
    x_oth, dg_oth = flip(x_own, "c", 1), flip(dg_other, "c", 1)
    parts = call(
        product_kernel,
        [shape(2, 144, D)] * 4 + [shape(288, D)] * 4,
        (x_own, x_oth, dg_own, dg_oth),
        6 * 10**9,
        20,
    )
    part_a, part_b = parts[:4], parts[4:]
    got_a, got_b = [], []
    for i, s in enumerate((1, 2, 3)):
        got_a.append(flip(part_a[s], "x", s))
        got_b.append(flip(part_b[(2, 1, 3)[i]], Y, (2, 1, 3)[i]))

    grad_in = call(
        grad_in_kernel,
        shape(512, 640),
        (place, dg_own, dg_other, prepared),
        3 * 10**9,
        20,
        scratch=[pltpu.VMEM((4, 864, D), BF), pltpu.VMEM((512, 640), BF), pltpu.SemaphoreType.DMA((5,))],
        specs=[SMEM, VMEM, VMEM, ANY],
    )

    sum_a = total(part_a[0], got_a).astype(BF).reshape(2, 2, 72, D)
    sum_b = total(part_b[0], got_b).astype(BF).reshape(4, 72, D)
    got_a, got_b = [], []
    for s in (2, 1, 3):
        got_a.append(flip(sum_a[s & 1, s >> 1], Y, s))
        got_b.append(flip(sum_b[s], "x", s))
    sum_a = total(sum_a[0, 0], got_a).reshape(4, 18, D)
    sum_b = total(sum_b[0], got_b).reshape(4, 18, D)
    got = [flip(jnp.concatenate([sum_a[i], sum_b[i]]).astype(BF), "z", s) for i, s in ((2, 6), (3, 7), (1, 1))]
    near = total(sum_a[0], [g[:18] for g in got])
    far = flip(total(sum_b[0], [g[18:] for g in got]).astype(BF), "z", 2)
    grad_wqkv = total(near[:, :864], [far[:, :864]])
    grad_wout = total(near[:, 864:], [far[:, 864:]])
    grad_in = lax.all_to_all(grad_in, FRAME, split_axis=0, concat_axis=0, tiled=True)
    (grad_in,) = call(unpack_kernel, [shape(ROWS, D)], (grad_in,), 10**9, 16)
    return grad_in.reshape(2, 128, D), grad_wqkv, grad_wout


def solution(mesh):
    fine = Mesh(mesh.devices.reshape(4, 8, 2, 2, 2), ("x", "z", "yh", "yl", "c"))
    patch = ("yl", "c")
    in_specs = (P(FRAME, patch, None), P(FRAME, patch, None), P(), P())
    out_specs = (P(FRAME, patch, None), P(FRAME, patch), P(FRAME, patch))
    return jax.shard_map(
        per_device, mesh=fine, in_specs=in_specs, out_specs=out_specs, check_vma=False
    )
```

```python
import jax
import jax.numpy as jnp
from jax import lax
from jax.experimental import pallas as pl
from jax.experimental.pallas import tpu as pltpu
from jax.sharding import Mesh, PartitionSpec as P

HEADS, HD, D = 16, 72, 1152
ROWS = 256
FRAME = ("x", "z", "yh")
Y = ("yh", "yl")
BF, F32 = jnp.bfloat16, jnp.float32
NN = ((1,), (0,))
NT = ((1,), (1,))
TN = ((0,), (0,))
VMEM = pl.BlockSpec(memory_space=pltpu.VMEM)
ANY = pl.BlockSpec(memory_space=pl.ANY)
SMEM = pl.BlockSpec(memory_space=pltpu.SMEM)
MIB = 1024 * 1024
CUTS = 2
TOGETHER = 4


def flip(array, axes, step):
    size = {"x": 4, "z": 8, Y: 4, "c": 2}[axes]
    return lax.ppermute(array, axes, [(i, i ^ step) for i in range(size)])


def mm(a, b, contract):
    return lax.dot_general(a, b, (contract, ((), ())), preferred_element_type=F32)


def pick(rows, cols, source):
    i = lax.broadcasted_iota(jnp.int32, (rows, cols), 0)
    j = lax.broadcasted_iota(jnp.int32, (rows, cols), 1)
    return (j == source(i)).astype(F32).astype(BF)


def pack_kernel(hidden, grad, out, held, sent, sems):
    loads = [pltpu.make_async_copy(array, held.at[i], sems.at[i]) for i, array in enumerate((hidden, grad))]
    for load in loads:
        load.start()
    at = lambda a: pick(
        512, ROWS, lambda i: jnp.where(((i >> 2) & 1) == a, ((i >> 1) & 1) * 128 + (i >> 3) * 2 + (i & 1), -1)
    )
    for load in loads:
        load.wait()
    sent[...] = (mm(at(0), held[0], NN) + mm(at(1), held[1], NN)).astype(BF)
    store = pltpu.make_async_copy(sent, out, sems.at[2])
    store.start()
    store.wait()


def column_order(place, start, count):
    x, z, yh = place[0], place[1], place[2]
    at = lax.broadcasted_iota(jnp.int32, (count, 1), 0) + start
    q = ((at.astype(F32) + 0.5) * (1.0 / 18)).astype(jnp.int32)
    first = q < 32
    rx = jnp.where(first, q >> 3, (q >> 2) & 3)
    ra = jnp.where(first, (q >> 2) & 1, (q >> 4) & 1)
    rz = ((q & 1) + 3 * (q & 2)) ^ jnp.where(first, 0, 2)
    return (x ^ rx) * 288 + (z ^ rz) * 36 + (yh ^ ra) * 18 + (at - 18 * q)


def slot(place, b):
    return ((b // 2) ^ place[3]) + 2 * ((b % 2) ^ place[4])


def prepare_kernel(place, w_qkv, w_out, out, held, made, sems):
    loads = [
        pltpu.make_async_copy(w_qkv.at[:, pl.ds(D * i, D)], held.at[i], sems.at[i]) for i in range(3)
    ] + [pltpu.make_async_copy(w_out, made.at[pl.ds(3 * D, D)], sems.at[3])]
    for load in loads:
        load.start()
    for i in range(3):
        order = column_order(place, 384 * i, 384)
        cols = lax.broadcasted_iota(jnp.int32, (384, D), 1)
        made[4 * D + 384 * i : 4 * D + 384 * (i + 1), :] = (cols == order).astype(F32).astype(BF)
    for i in range(3):
        loads[i].wait()
        for j in range(3):
            made[D * i + 384 * j : D * i + 384 * (j + 1), :] = held[i, :, 384 * j : 384 * (j + 1)].T
    loads[3].wait()
    store = pltpu.make_async_copy(made, out.at[pl.ds(0, 5 * D)], sems.at[4])
    store.start()
    store.wait()


def attend_kernel(home, got, prepared, x_out, dg_own, dg_other, weights, sems, qkv_t, do_t, dqkv_t, attn_t):
    order = (3, 0, 1, 2, 4)
    loads = [pltpu.make_async_copy(prepared.at[pl.ds(D * i, D)], weights.at[i], sems.at[i]) for i in order]
    for load in loads:
        load.start()
    place = lambda a: lambda i: ((i >> 1) & 63) * 8 + a * 4 + (i & 1) * 2 + (i >> 7)
    gout = mm(pick(ROWS, 512, place(1)), got[...], NN).astype(BF)
    hid = mm(pick(ROWS, 512, place(0)), got[...], NN).astype(BF)
    loads[0].wait()
    for i in range(3):
        cut = slice(384 * i, 384 * (i + 1))
        do_t[cut, :] = mm(weights[3, cut, :], gout, NT).astype(BF).astype(F32)
    for i in range(3):
        loads[1 + i].wait()
        for j in range(3):
            part = mm(weights[i, 384 * j : 384 * (j + 1), :], hid, NT)
            qkv_t[D * i + 384 * j : D * i + 384 * (j + 1), :] = part.astype(BF).astype(F32)

    def keep(b, rows, at):
        @pl.when(slot(home, b) < 2)
        def _():
            dg_own[slot(home, b) & 1, at, :] = rows

        @pl.when(slot(home, b) >= 2)
        def _():
            dg_other[slot(home, b) & 1, at, :] = rows

    gout_t = gout.T
    for b in range(4):
        keep(b, gout_t[288 * b : 288 * (b + 1)], slice(864, D))

    scale = 1.0 / HD**0.5

    def heads(t, carry):
        at = lambda i, h: pl.ds(pl.multiple_of(D * i + HD * (t * TOGETHER + h), 8), HD)
        pairs = []
        for h in range(TOGETHER):
            q_t, k_t, v_t = (qkv_t[at(i, h), :].astype(BF) for i in range(3))
            d_t = do_t[at(0, h), :].astype(BF)
            for p in range(2):
                cut = slice(128 * p, 128 * (p + 1))
                pairs.append((h, cut, q_t[:, cut], k_t[:, cut], v_t[:, cut], d_t[:, cut]))
        scores = [mm(k, q, TN) * scale for h, cut, q, k, v, do in pairs]
        dprobs = [mm(v, do, TN) for h, cut, q, k, v, do in pairs]
        probs = []
        for s in scores:
            grown = jnp.exp(s - jnp.max(s, axis=0, keepdims=True))
            probs.append(grown * (1.0 / jnp.sum(grown, axis=0, keepdims=True)))
        probs_b = [p.astype(BF) for p in probs]
        dscores = [(p * (d - jnp.sum(p * d, axis=0, keepdims=True)) * scale).astype(BF) for p, d in zip(probs, dprobs)]
        for (h, cut, q, k, v, do), p in zip(pairs, probs_b):
            attn_t[at(0, h), cut] = mm(v, p, NN)
            dqkv_t[at(2, h), cut] = mm(do, p, NT)
        for (h, cut, q, k, v, do), d in zip(pairs, dscores):
            dqkv_t[at(0, h), cut] = mm(k, d, NN)
            dqkv_t[at(1, h), cut] = mm(q, d, NT)
        return carry

    lax.fori_loop(0, HEADS // TOGETHER, heads, 0, unroll=4)

    attn = attn_t[...].astype(BF)
    loads[4].wait()
    for i in range(3):
        chosen = weights[4, 384 * i : 384 * (i + 1), :]
        x_out[384 * i : 384 * (i + 1), :] = mm(chosen, hid, NT).astype(BF)
        x_out[D + 384 * i : D + 384 * (i + 1), :] = mm(chosen, attn, NN).astype(BF)
    for b in range(4):
        keep(b, dqkv_t[864 * b : 864 * (b + 1), :].astype(BF), slice(0, 864))


def grad_in_kernel(home, dg_own, dg_other, prepared, out, w_t, sent, sems):
    loads = [pltpu.make_async_copy(prepared.at[pl.ds(864 * i, 864)], w_t.at[i], sems.at[i]) for i in range(4)]
    for load in loads:
        load.start()
    total = None
    for b in range(4):
        kept = dg_own[slot(home, b) & 1, :864, :]
        away = dg_other[slot(home, b) & 1, :864, :]
        rows = jnp.where(slot(home, b) < 2, kept, away)
        loads[b].wait()
        part = mm(rows, w_t[b], TN)
        total = part if total is None else total + part
    total = total.astype(BF)
    at = lambda a: pick(
        512, ROWS, lambda i: jnp.where(((i >> 2) & 1) == a, (i & 1) * 128 + (i >> 3) * 2 + ((i >> 1) & 1), -1)
    )
    sent[...] = (mm(at(0), total[:, :640], NN) + mm(at(1), total[:, 512:], NN)).astype(BF)
    store = pltpu.make_async_copy(sent, out, sems.at[4])
    store.start()
    store.wait()


def unpack_kernel(got, out):
    recv = got[...]
    at = lambda a: pick(ROWS, 512, lambda i: ((i >> 1) & 63) * 8 + a * 4 + (i >> 7) * 2 + (i & 1))
    out[:, :640] = mm(at(0), recv, NN).astype(BF)
    out[:, 640:] = mm(at(1), recv[:, 128:], NN).astype(BF)


def product_kernel(x_own, x_oth, dg_own, dg_oth, *parts):
    row = lax.broadcasted_iota(jnp.int32, (128, 2 * ROWS), 0)
    both = lambda at: jnp.concatenate([x_own[at, :], x_oth[at, :]], axis=1)
    for r in range(2):
        d_all = jnp.concatenate([dg_own[r], dg_oth[r]], axis=1)
        edge = d_all[768:896]
        none = jnp.zeros_like(edge)
        edge = jnp.concatenate([jnp.where(row < 96, edge, none), jnp.where(row < 96, none, edge)], axis=1)
        for s in range(0, 8, 8 // CUTS):
            rows = D // CUTS
            hid = both(slice(144 * s, 144 * s + rows))
            attn = both(slice(D + 144 * s, D + 144 * s + rows))
            pieces = [
                (0, mm(hid, d_all[:384], NT)),
                (384, mm(hid, d_all[384:768], NT)),
                (768, mm(jnp.concatenate([hid, attn], axis=1), edge, NT)),
                (896, mm(attn, d_all[896:], NT)),
            ]
            for lo, piece in pieces:
                cols = slice(lo, lo + piece.shape[1])
                piece = piece.astype(BF)
                for t in range(8 // CUTS):
                    part = piece[144 * t : 144 * (t + 1)]
                    if s + t < 4:
                        parts[s + t][r, :, cols] = part
                    else:
                        ra, half = divmod(s + t - 4, 2)
                        parts[4 + 2 * ra + r][144 * half : 144 * (half + 1), cols] = part


def shape(*dims, dtype=BF):
    return jax.ShapeDtypeStruct(dims, dtype)


def call(kernel, outs, ins, flops, mib, scratch=(), specs=None):
    return pl.pallas_call(
        kernel,
        out_shape=outs,
        in_specs=specs or [VMEM] * len(ins),
        out_specs=[VMEM] * len(outs) if isinstance(outs, list) else ANY,
        scratch_shapes=list(scratch),
        compiler_params=pltpu.CompilerParams(vmem_limit_bytes=mib * MIB),
        cost_estimate=pl.CostEstimate(flops=flops, bytes_accessed=10**7, transcendentals=0),
    )(*ins)


def prepare_call(place, w_qkv, w_out):
    return call(
        prepare_kernel,
        shape(14 * D, D),
        (place, w_qkv, w_out),
        10**9,
        32,
        scratch=[pltpu.VMEM((3, D, D), BF), pltpu.VMEM((5 * D, D), BF), pltpu.SemaphoreType.DMA((5,))],
        specs=[SMEM, ANY, ANY],
    )


def attend_call(place, both, prepared):
    return call(
        attend_kernel,
        [shape(2 * D, ROWS), shape(2, D, ROWS), shape(2, D, ROWS)],
        (place, both, prepared),
        10 * 10**9,
        28,
        scratch=[
            pltpu.VMEM((5, D, D), BF),
            pltpu.SemaphoreType.DMA((5,)),
            pltpu.VMEM((3 * D, ROWS), F32),
            pltpu.VMEM((D, ROWS), F32),
            pltpu.VMEM((3 * D, ROWS), F32),
            pltpu.VMEM((D, ROWS), F32),
        ],
        specs=[SMEM, VMEM, ANY],
    )


def total(own, others):
    return own.astype(F32) + sum(g.astype(F32) for g in others)


def per_device(hidden_in, grad_out, w_qkv, w_out):
    place = jnp.stack([lax.axis_index(a) for a in ("x", "z", "yh", "yl", "c")]).astype(jnp.int32)
    both = call(
        pack_kernel,
        shape(512, D),
        (hidden_in.reshape(ROWS, D), grad_out.reshape(ROWS, D)),
        10**9,
        58,
        scratch=[pltpu.VMEM((2, ROWS, D), BF), pltpu.VMEM((512, D), BF), pltpu.SemaphoreType.DMA((3,))],
        specs=[ANY, ANY],
    )
    both = lax.all_to_all(both, FRAME, split_axis=0, concat_axis=0, tiled=True)
    prepared = prepare_call(place, w_qkv, w_out)
    x_own, dg_own, dg_other = attend_call(place, both, prepared)
    x_oth, dg_oth = flip(x_own, "c", 1), flip(dg_other, "c", 1)
    parts = call(
        product_kernel,
        [shape(2, 144, D)] * 4 + [shape(288, D)] * 4,
        (x_own, x_oth, dg_own, dg_oth),
        6 * 10**9,
        20,
    )
    part_a, part_b = parts[:4], parts[4:]
    got_a, got_b = [], []
    for i, s in enumerate((1, 2, 3)):
        got_a.append(flip(part_a[s], "x", s))
        got_b.append(flip(part_b[(2, 1, 3)[i]], Y, (2, 1, 3)[i]))

    dg_own, dg_other, _ = lax.optimization_barrier((dg_own, dg_other, got_a[0]))
    grad_in = call(
        grad_in_kernel,
        shape(512, 640),
        (place, dg_own, dg_other, prepared),
        3 * 10**9,
        20,
        scratch=[pltpu.VMEM((4, 864, D), BF), pltpu.VMEM((512, 640), BF), pltpu.SemaphoreType.DMA((5,))],
        specs=[SMEM, VMEM, VMEM, ANY],
    )

    sum_a = total(part_a[0], got_a).astype(BF).reshape(2, 2, 72, D)
    sum_b = total(part_b[0], got_b).astype(BF).reshape(4, 72, D)
    got_a, got_b = [], []
    for s in (2, 1, 3):
        got_a.append(flip(sum_a[s & 1, s >> 1], Y, s))
        got_b.append(flip(sum_b[s], "x", s))
    sum_a = total(sum_a[0, 0], got_a).reshape(4, 18, D)
    sum_b = total(sum_b[0], got_b).reshape(4, 18, D)
    got = [flip(jnp.concatenate([sum_a[i], sum_b[i]]).astype(BF), "z", s) for i, s in ((2, 6), (3, 7), (1, 1))]
    near = total(sum_a[0], [g[:18] for g in got])
    far = flip(total(sum_b[0], [g[18:] for g in got]).astype(BF), "z", 2)
    grad_wqkv = total(near[:, :864], [far[:, :864]])
    grad_wout = total(near[:, 864:], [far[:, 864:]])
    grad_in = lax.all_to_all(grad_in, FRAME, split_axis=0, concat_axis=0, tiled=True)
    (grad_in,) = call(unpack_kernel, [shape(ROWS, D)], (grad_in,), 10**9, 16)
    return grad_in.reshape(2, 128, D), grad_wqkv, grad_wout


def solution(mesh):
    fine = Mesh(mesh.devices.reshape(4, 8, 2, 2, 2), ("x", "z", "yh", "yl", "c"))
    patch = ("yl", "c")
    in_specs = (P(FRAME, patch, None), P(FRAME, patch, None), P(), P())
    out_specs = (P(FRAME, patch, None), P(FRAME, patch), P(FRAME, patch))
    return jax.shard_map(
        per_device, mesh=fine, in_specs=in_specs, out_specs=out_specs, check_vma=False
    )
```

```python
import jax
import jax.numpy as jnp
from jax import lax
from jax.experimental import pallas as pl
from jax.experimental.pallas import tpu as pltpu
from jax.sharding import Mesh, PartitionSpec as P

HEADS, HD, D = 16, 72, 1152
ROWS = 256
FRAME = ("x", "z", "yh")
Y = ("yh", "yl")
BF, F32 = jnp.bfloat16, jnp.float32
NN = ((1,), (0,))
NT = ((1,), (1,))
TN = ((0,), (0,))
VMEM = pl.BlockSpec(memory_space=pltpu.VMEM)
ANY = pl.BlockSpec(memory_space=pl.ANY)
SMEM = pl.BlockSpec(memory_space=pltpu.SMEM)
MIB = 1024 * 1024
CUTS = 2
TOGETHER = 4


def flip(array, axes, step):
    size = {"x": 4, "z": 8, Y: 4, "c": 2}[axes]
    return lax.ppermute(array, axes, [(i, i ^ step) for i in range(size)])


def mm(a, b, contract):
    return lax.dot_general(a, b, (contract, ((), ())), preferred_element_type=F32)


def pick(rows, cols, source):
    i = lax.broadcasted_iota(jnp.int32, (rows, cols), 0)
    j = lax.broadcasted_iota(jnp.int32, (rows, cols), 1)
    return (j == source(i)).astype(F32).astype(BF)


def pack_kernel(hidden, grad, out, held, sent, sems):
    loads = [pltpu.make_async_copy(array, held.at[i], sems.at[i]) for i, array in enumerate((hidden, grad))]
    for load in loads:
        load.start()
    from_row = lambda i: ((i >> 2) & 1) * 256 + ((i >> 1) & 1) * 128 + (i >> 3) * 2 + (i & 1)
    chosen = [pick(ROWS, 512, lambda i: from_row(i + ROWS * half)) for half in range(2)]
    for load in loads:
        load.wait()
    rows = jnp.concatenate([held[0], held[1]], axis=0)
    stores = []
    for half in range(2):
        cut = pl.ds(ROWS * half, ROWS)
        sent[cut, :] = mm(chosen[half], rows, NN).astype(BF)
        stores.append(pltpu.make_async_copy(sent.at[cut], out.at[cut], sems.at[2 + half]))
        stores[half].start()
    for store in stores:
        store.wait()


def column_order(place, start, count):
    x, z, yh = place[0], place[1], place[2]
    at = lax.broadcasted_iota(jnp.int32, (count, 1), 0) + start
    q = ((at.astype(F32) + 0.5) * (1.0 / 18)).astype(jnp.int32)
    first = q < 32
    rx = jnp.where(first, q >> 3, (q >> 2) & 3)
    ra = jnp.where(first, (q >> 2) & 1, (q >> 4) & 1)
    rz = ((q & 1) + 3 * (q & 2)) ^ jnp.where(first, 0, 2)
    return (x ^ rx) * 288 + (z ^ rz) * 36 + (yh ^ ra) * 18 + (at - 18 * q)


def slot(place, b):
    return ((b // 2) ^ place[3]) + 2 * ((b % 2) ^ place[4])


def prepare_kernel(place, w_qkv, w_out, out, held, made, sems):
    loads = [
        pltpu.make_async_copy(w_qkv.at[:, pl.ds(D * i, D)], held.at[i], sems.at[i]) for i in range(3)
    ] + [pltpu.make_async_copy(w_out, made.at[pl.ds(3 * D, D)], sems.at[3])]
    for load in loads:
        load.start()
    for i in range(3):
        order = column_order(place, 384 * i, 384)
        cols = lax.broadcasted_iota(jnp.int32, (384, D), 1)
        made[4 * D + 384 * i : 4 * D + 384 * (i + 1), :] = (cols == order).astype(F32).astype(BF)
    for i in range(3):
        loads[i].wait()
        for j in range(3):
            made[D * i + 384 * j : D * i + 384 * (j + 1), :] = held[i, :, 384 * j : 384 * (j + 1)].T
    loads[3].wait()
    store = pltpu.make_async_copy(made, out.at[pl.ds(0, 5 * D)], sems.at[4])
    store.start()
    store.wait()


def attend_kernel(home, got, prepared, x_out, dg_own, dg_other, weights, sems, qkv_t, do_t, dqkv_t, attn_t):
    order = (3, 0, 1, 2, 4)
    loads = [pltpu.make_async_copy(prepared.at[pl.ds(D * i, D)], weights.at[i], sems.at[i]) for i in order]
    for load in loads:
        load.start()
    from_row = lambda i: ((i >> 1) & 63) * 8 + (i >> 8) * 4 + (i & 1) * 2 + ((i >> 7) & 1)
    moved = mm(pick(512, 512, from_row), got[...], NN).astype(BF)
    hid, gout = moved[:ROWS], moved[ROWS:]
    loads[0].wait()
    for i in range(3):
        cut = slice(384 * i, 384 * (i + 1))
        do_t[cut, :] = mm(weights[3, cut, :], gout, NT).astype(BF).astype(F32)
    for i in range(3):
        loads[1 + i].wait()
        for j in range(3):
            part = mm(weights[i, 384 * j : 384 * (j + 1), :], hid, NT)
            qkv_t[D * i + 384 * j : D * i + 384 * (j + 1), :] = part.astype(BF).astype(F32)

    def keep(b, rows, at):
        @pl.when(slot(home, b) < 2)
        def _():
            dg_own[slot(home, b) & 1, at, :] = rows

        @pl.when(slot(home, b) >= 2)
        def _():
            dg_other[slot(home, b) & 1, at, :] = rows

    gout_t = gout.T
    for b in range(4):
        keep(b, gout_t[288 * b : 288 * (b + 1)], slice(864, D))

    scale = 1.0 / HD**0.5

    def heads(t, carry):
        at = lambda i, h: pl.ds(pl.multiple_of(D * i + HD * (t * TOGETHER + h), 8), HD)
        pairs = []
        for h in range(TOGETHER):
            q_t, k_t, v_t = (qkv_t[at(i, h), :].astype(BF) for i in range(3))
            d_t = do_t[at(0, h), :].astype(BF)
            for p in range(2):
                cut = slice(128 * p, 128 * (p + 1))
                pairs.append((h, cut, q_t[:, cut], k_t[:, cut], v_t[:, cut], d_t[:, cut]))
        scores = [mm(k, q, TN) * scale for h, cut, q, k, v, do in pairs]
        dprobs = [mm(v, do, TN) for h, cut, q, k, v, do in pairs]
        probs = []
        for s in scores:
            grown = jnp.exp(s - jnp.max(s, axis=0, keepdims=True))
            probs.append(grown * (1.0 / jnp.sum(grown, axis=0, keepdims=True)))
        probs_b = [p.astype(BF) for p in probs]
        dscores = [(p * (d - jnp.sum(p * d, axis=0, keepdims=True)) * scale).astype(BF) for p, d in zip(probs, dprobs)]
        for (h, cut, q, k, v, do), p in zip(pairs, probs_b):
            attn_t[at(0, h), cut] = mm(v, p, NN)
            dqkv_t[at(2, h), cut] = mm(do, p, NT)
        for (h, cut, q, k, v, do), d in zip(pairs, dscores):
            dqkv_t[at(0, h), cut] = mm(k, d, NN)
            dqkv_t[at(1, h), cut] = mm(q, d, NT)
        return carry

    lax.fori_loop(0, HEADS // TOGETHER, heads, 0, unroll=4)

    attn = attn_t[...].astype(BF)
    loads[4].wait()
    for i in range(3):
        chosen = weights[4, 384 * i : 384 * (i + 1), :]
        x_out[384 * i : 384 * (i + 1), :] = mm(chosen, hid, NT).astype(BF)
        x_out[D + 384 * i : D + 384 * (i + 1), :] = mm(chosen, attn, NN).astype(BF)
    for b in range(4):
        keep(b, dqkv_t[864 * b : 864 * (b + 1), :].astype(BF), slice(0, 864))


def grad_in_kernel(home, dg_own, dg_other, prepared, out, w_t, sent, sems):
    loads = [pltpu.make_async_copy(prepared.at[pl.ds(864 * i, 864)], w_t.at[i], sems.at[i]) for i in range(4)]
    for load in loads:
        load.start()
    total = None
    for b in range(4):
        kept = dg_own[slot(home, b) & 1, :864, :]
        away = dg_other[slot(home, b) & 1, :864, :]
        rows = jnp.where(slot(home, b) < 2, kept, away)
        loads[b].wait()
        part = mm(rows, w_t[b], TN)
        total = part if total is None else total + part
    total = total.astype(BF)
    from_row = lambda i: ((i >> 2) & 1) * 256 + (i & 1) * 128 + (i >> 3) * 2 + ((i >> 1) & 1)
    columns = jnp.concatenate([total[:, :640], total[:, 512:]], axis=0)
    sent[...] = mm(pick(512, 512, from_row), columns, NN).astype(BF)
    store = pltpu.make_async_copy(sent, out, sems.at[4])
    store.start()
    store.wait()


def unpack_kernel(got, out):
    recv = got[...]
    at = lambda a: pick(ROWS, 512, lambda i: ((i >> 1) & 63) * 8 + a * 4 + (i >> 7) * 2 + (i & 1))
    out[:, :640] = mm(at(0), recv, NN).astype(BF)
    out[:, 640:] = mm(at(1), recv[:, 128:], NN).astype(BF)


def product_kernel(x_own, x_oth, dg_own, dg_oth, *parts):
    row = lax.broadcasted_iota(jnp.int32, (128, 2 * ROWS), 0)
    both = lambda at: jnp.concatenate([x_own[at, :], x_oth[at, :]], axis=1)
    for r in range(2):
        d_all = jnp.concatenate([dg_own[r], dg_oth[r]], axis=1)
        edge = d_all[768:896]
        none = jnp.zeros_like(edge)
        edge = jnp.concatenate([jnp.where(row < 96, edge, none), jnp.where(row < 96, none, edge)], axis=1)
        for s in range(0, 8, 8 // CUTS):
            rows = D // CUTS
            hid = both(slice(144 * s, 144 * s + rows))
            attn = both(slice(D + 144 * s, D + 144 * s + rows))
            pieces = [
                (0, mm(hid, d_all[:384], NT)),
                (384, mm(hid, d_all[384:768], NT)),
                (768, mm(jnp.concatenate([hid, attn], axis=1), edge, NT)),
                (896, mm(attn, d_all[896:], NT)),
            ]
            for lo, piece in pieces:
                cols = slice(lo, lo + piece.shape[1])
                piece = piece.astype(BF)
                for t in range(8 // CUTS):
                    part = piece[144 * t : 144 * (t + 1)]
                    if s + t < 4:
                        parts[s + t][r, :, cols] = part
                    else:
                        ra, half = divmod(s + t - 4, 2)
                        parts[4 + 2 * ra + r][144 * half : 144 * (half + 1), cols] = part


def shape(*dims, dtype=BF):
    return jax.ShapeDtypeStruct(dims, dtype)


def call(kernel, outs, ins, flops, mib, scratch=(), specs=None):
    return pl.pallas_call(
        kernel,
        out_shape=outs,
        in_specs=specs or [VMEM] * len(ins),
        out_specs=[VMEM] * len(outs) if isinstance(outs, list) else ANY,
        scratch_shapes=list(scratch),
        compiler_params=pltpu.CompilerParams(vmem_limit_bytes=mib * MIB),
        cost_estimate=pl.CostEstimate(flops=flops, bytes_accessed=10**7, transcendentals=0),
    )(*ins)


def prepare_call(place, w_qkv, w_out):
    return call(
        prepare_kernel,
        shape(14 * D, D),
        (place, w_qkv, w_out),
        10**9,
        32,
        scratch=[pltpu.VMEM((3, D, D), BF), pltpu.VMEM((5 * D, D), BF), pltpu.SemaphoreType.DMA((5,))],
        specs=[SMEM, ANY, ANY],
    )


def attend_call(place, both, prepared):
    return call(
        attend_kernel,
        [shape(2 * D, ROWS), shape(2, D, ROWS), shape(2, D, ROWS)],
        (place, both, prepared),
        10 * 10**9,
        28,
        scratch=[
            pltpu.VMEM((5, D, D), BF),
            pltpu.SemaphoreType.DMA((5,)),
            pltpu.VMEM((3 * D, ROWS), F32),
            pltpu.VMEM((D, ROWS), F32),
            pltpu.VMEM((3 * D, ROWS), F32),
            pltpu.VMEM((D, ROWS), F32),
        ],
        specs=[SMEM, VMEM, ANY],
    )


def total(own, others):
    return own.astype(F32) + sum(g.astype(F32) for g in others)


def per_device(hidden_in, grad_out, w_qkv, w_out):
    place = jnp.stack([lax.axis_index(a) for a in ("x", "z", "yh", "yl", "c")]).astype(jnp.int32)
    both = call(
        pack_kernel,
        shape(512, D),
        (hidden_in.reshape(ROWS, D), grad_out.reshape(ROWS, D)),
        10**9,
        58,
        scratch=[pltpu.VMEM((2, ROWS, D), BF), pltpu.VMEM((512, D), BF), pltpu.SemaphoreType.DMA((4,))],
        specs=[ANY, ANY],
    )
    both = lax.all_to_all(both, FRAME, split_axis=0, concat_axis=0, tiled=True)
    prepared = prepare_call(place, w_qkv, w_out)
    x_own, dg_own, dg_other = attend_call(place, both, prepared)
    x_oth, dg_oth = flip(x_own, "c", 1), flip(dg_other, "c", 1)
    parts = call(
        product_kernel,
        [shape(2, 144, D)] * 4 + [shape(288, D)] * 4,
        (x_own, x_oth, dg_own, dg_oth),
        6 * 10**9,
        20,
    )
    part_a, part_b = parts[:4], parts[4:]
    got_a, got_b = [], []
    for i, s in enumerate((1, 2, 3)):
        got_a.append(flip(part_a[s], "x", s))
        got_b.append(flip(part_b[(2, 1, 3)[i]], Y, (2, 1, 3)[i]))

    dg_own, dg_other, _ = lax.optimization_barrier((dg_own, dg_other, got_a[0]))
    grad_in = call(
        grad_in_kernel,
        shape(512, 640),
        (place, dg_own, dg_other, prepared),
        3 * 10**9,
        20,
        scratch=[pltpu.VMEM((4, 864, D), BF), pltpu.VMEM((512, 640), BF), pltpu.SemaphoreType.DMA((5,))],
        specs=[SMEM, VMEM, VMEM, ANY],
    )

    sum_a = total(part_a[0], got_a).astype(BF).reshape(2, 2, 72, D)
    sum_b = total(part_b[0], got_b).astype(BF).reshape(4, 72, D)
    got_a, got_b = [], []
    for s in (2, 1, 3):
        got_a.append(flip(sum_a[s & 1, s >> 1], Y, s))
        got_b.append(flip(sum_b[s], "x", s))
    sum_a = total(sum_a[0, 0], got_a).reshape(4, 18, D)
    sum_b = total(sum_b[0], got_b).reshape(4, 18, D)
    got = [flip(jnp.concatenate([sum_a[i], sum_b[i]]).astype(BF), "z", s) for i, s in ((2, 6), (3, 7), (1, 1))]
    near = total(sum_a[0], [g[:18] for g in got])
    grad_in = lax.all_to_all(grad_in, FRAME, split_axis=0, concat_axis=0, tiled=True)
    (grad_in,) = call(unpack_kernel, [shape(ROWS, D)], (grad_in,), 10**9, 16)
    near, grad_in = lax.optimization_barrier((near, grad_in))
    far = flip(total(sum_b[0], [g[18:] for g in got]).astype(BF), "z", 2)
    grad_wqkv = total(near[:, :864], [far[:, :864]])
    grad_wout = total(near[:, 864:], [far[:, 864:]])
    return grad_in.reshape(2, 128, D), grad_wqkv, grad_wout


def solution(mesh):
    fine = Mesh(mesh.devices.reshape(4, 8, 2, 2, 2), ("x", "z", "yh", "yl", "c"))
    patch = ("yl", "c")
    in_specs = (P(FRAME, patch, None), P(FRAME, patch, None), P(), P())
    out_specs = (P(FRAME, patch, None), P(FRAME, patch), P(FRAME, patch))
    return jax.shard_map(
        per_device, mesh=fine, in_specs=in_specs, out_specs=out_specs, check_vma=False
    )
```

```python
import jax
import jax.numpy as jnp
from jax import lax
from jax.experimental import pallas as pl
from jax.experimental.pallas import tpu as pltpu
from jax.sharding import Mesh, PartitionSpec as P

HEADS, HD, D = 16, 72, 1152
ROWS = 256
FRAME = ("x", "z", "yh")
Y = ("yh", "yl")
BF, F32 = jnp.bfloat16, jnp.float32
NN = ((1,), (0,))
NT = ((1,), (1,))
TN = ((0,), (0,))
VMEM = pl.BlockSpec(memory_space=pltpu.VMEM)
ANY = pl.BlockSpec(memory_space=pl.ANY)
SMEM = pl.BlockSpec(memory_space=pltpu.SMEM)
MIB = 1024 * 1024
CUTS = 1
TOGETHER = 4


def flip(array, axes, step):
    size = {"x": 4, "z": 8, Y: 4, "c": 2}[axes]
    return lax.ppermute(array, axes, [(i, i ^ step) for i in range(size)])


def mm(a, b, contract):
    return lax.dot_general(a, b, (contract, ((), ())), preferred_element_type=F32)


def pick(rows, cols, source):
    i = lax.broadcasted_iota(jnp.int32, (rows, cols), 0)
    j = lax.broadcasted_iota(jnp.int32, (rows, cols), 1)
    return (j == source(i)).astype(F32).astype(BF)


def pack_kernel(hidden, grad, out, held, sent, sems):
    loads = [pltpu.make_async_copy(array, held.at[i], sems.at[i]) for i, array in enumerate((hidden, grad))]
    for load in loads:
        load.start()
    from_row = lambda i: ((i >> 2) & 1) * 256 + ((i >> 1) & 1) * 128 + (i >> 3) * 2 + (i & 1)
    chosen = [pick(ROWS, 512, lambda i: from_row(i + ROWS * half)) for half in range(2)]
    for load in loads:
        load.wait()
    rows = jnp.concatenate([held[0], held[1]], axis=0)
    stores = []
    for half in range(2):
        cut = pl.ds(ROWS * half, ROWS)
        sent[cut, :] = mm(chosen[half], rows, NN).astype(BF)
        stores.append(pltpu.make_async_copy(sent.at[cut], out.at[cut], sems.at[2 + half]))
        stores[half].start()
    for store in stores:
        store.wait()


def column_order(place, start, count):
    x, z, yh = place[0], place[1], place[2]
    at = lax.broadcasted_iota(jnp.int32, (count, 1), 0) + start
    q = ((at.astype(F32) + 0.5) * (1.0 / 18)).astype(jnp.int32)
    first = q < 32
    rx = jnp.where(first, q >> 3, (q >> 2) & 3)
    ra = jnp.where(first, (q >> 2) & 1, (q >> 4) & 1)
    rz = ((q & 1) + 3 * (q & 2)) ^ jnp.where(first, 0, 2)
    return (x ^ rx) * 288 + (z ^ rz) * 36 + (yh ^ ra) * 18 + (at - 18 * q)


def slot(place, b):
    return ((b // 2) ^ place[3]) + 2 * ((b % 2) ^ place[4])


def prepare_kernel(place, w_qkv, w_out, out, held, made, sems):
    loads = [
        pltpu.make_async_copy(w_qkv.at[:, pl.ds(D * i, D)], held.at[i], sems.at[i]) for i in range(3)
    ] + [pltpu.make_async_copy(w_out, made.at[pl.ds(3 * D, D)], sems.at[3])]
    for load in loads:
        load.start()
    for i in range(3):
        order = column_order(place, 384 * i, 384)
        cols = lax.broadcasted_iota(jnp.int32, (384, D), 1)
        made[4 * D + 384 * i : 4 * D + 384 * (i + 1), :] = (cols == order).astype(F32).astype(BF)
    for i in range(3):
        loads[i].wait()
        for j in range(3):
            made[D * i + 384 * j : D * i + 384 * (j + 1), :] = held[i, :, 384 * j : 384 * (j + 1)].T
    loads[3].wait()
    store = pltpu.make_async_copy(made, out.at[pl.ds(0, 5 * D)], sems.at[4])
    store.start()
    store.wait()


def attend_kernel(home, got, prepared, x_out, dg_own, dg_other, weights, sems, qkv_t, do_t, dqkv_t, attn_t):
    order = (3, 0, 1, 2, 4)
    loads = [pltpu.make_async_copy(prepared.at[pl.ds(D * i, D)], weights.at[i], sems.at[i]) for i in order]
    for load in loads:
        load.start()
    from_row = lambda i: ((i >> 1) & 63) * 8 + (i >> 8) * 4 + (i & 1) * 2 + ((i >> 7) & 1)
    moved = mm(pick(512, 512, from_row), got[...], NN).astype(BF)
    hid, gout = moved[:ROWS], moved[ROWS:]
    loads[0].wait()
    for i in range(3):
        cut = slice(384 * i, 384 * (i + 1))
        do_t[cut, :] = mm(weights[3, cut, :], gout, NT).astype(BF).astype(F32)
    for i in range(3):
        loads[1 + i].wait()
        for j in range(3):
            part = mm(weights[i, 384 * j : 384 * (j + 1), :], hid, NT)
            qkv_t[D * i + 384 * j : D * i + 384 * (j + 1), :] = part.astype(BF).astype(F32)

    def keep(b, rows, at):
        @pl.when(slot(home, b) < 2)
        def _():
            dg_own[slot(home, b) & 1, at, :] = rows

        @pl.when(slot(home, b) >= 2)
        def _():
            dg_other[slot(home, b) & 1, at, :] = rows

    gout_t = gout.T
    for b in range(4):
        keep(b, gout_t[288 * b : 288 * (b + 1)], slice(864, D))

    scale = 1.0 / HD**0.5

    def heads(t, carry):
        at = lambda i, h: pl.ds(pl.multiple_of(D * i + HD * (t * TOGETHER + h), 8), HD)
        pairs = []
        for h in range(TOGETHER):
            q_t, k_t, v_t = (qkv_t[at(i, h), :].astype(BF) for i in range(3))
            d_t = do_t[at(0, h), :].astype(BF)
            for p in range(2):
                cut = slice(128 * p, 128 * (p + 1))
                pairs.append((h, cut, q_t[:, cut], k_t[:, cut], v_t[:, cut], d_t[:, cut]))
        scores = [mm(k, q, TN) * scale for h, cut, q, k, v, do in pairs]
        dprobs = [mm(v, do, TN) for h, cut, q, k, v, do in pairs]
        probs = []
        for s in scores:
            grown = jnp.exp(s - jnp.max(s, axis=0, keepdims=True))
            probs.append(grown * (1.0 / jnp.sum(grown, axis=0, keepdims=True)))
        probs_b = [p.astype(BF) for p in probs]
        dscores = [(p * (d - jnp.sum(p * d, axis=0, keepdims=True)) * scale).astype(BF) for p, d in zip(probs, dprobs)]
        for (h, cut, q, k, v, do), p in zip(pairs, probs_b):
            attn_t[at(0, h), cut] = mm(v, p, NN)
            dqkv_t[at(2, h), cut] = mm(do, p, NT)
        for (h, cut, q, k, v, do), d in zip(pairs, dscores):
            dqkv_t[at(0, h), cut] = mm(k, d, NN)
            dqkv_t[at(1, h), cut] = mm(q, d, NT)
        return carry

    lax.fori_loop(0, HEADS // TOGETHER, heads, 0, unroll=4)

    attn = attn_t[...].astype(BF)
    loads[4].wait()
    for i in range(3):
        chosen = weights[4, 384 * i : 384 * (i + 1), :]
        x_out[384 * i : 384 * (i + 1), :] = mm(chosen, hid, NT).astype(BF)
        x_out[D + 384 * i : D + 384 * (i + 1), :] = mm(chosen, attn, NN).astype(BF)
    for b in range(4):
        keep(b, dqkv_t[864 * b : 864 * (b + 1), :].astype(BF), slice(0, 864))


def grad_in_kernel(home, dg_own, dg_other, prepared, out, w_t, sent, sems):
    loads = [pltpu.make_async_copy(prepared.at[pl.ds(864 * i, 864)], w_t.at[i], sems.at[i]) for i in range(4)]
    for load in loads:
        load.start()
    total = None
    for b in range(4):
        kept = dg_own[slot(home, b) & 1, :864, :]
        away = dg_other[slot(home, b) & 1, :864, :]
        rows = jnp.where(slot(home, b) < 2, kept, away)
        loads[b].wait()
        part = mm(rows, w_t[b], TN)
        total = part if total is None else total + part
    total = total.astype(BF)
    from_row = lambda i: ((i >> 2) & 1) * 256 + (i & 1) * 128 + (i >> 3) * 2 + ((i >> 1) & 1)
    columns = jnp.concatenate([total[:, :640], total[:, 512:]], axis=0)
    sent[...] = mm(pick(512, 512, from_row), columns, NN).astype(BF)
    store = pltpu.make_async_copy(sent, out, sems.at[4])
    store.start()
    store.wait()


def unpack_kernel(got, out):
    recv = got[...]
    at = lambda a: pick(ROWS, 512, lambda i: ((i >> 1) & 63) * 8 + a * 4 + (i >> 7) * 2 + (i & 1))
    out[:, :640] = mm(at(0), recv, NN).astype(BF)
    out[:, 640:] = mm(at(1), recv[:, 128:], NN).astype(BF)


def product_kernel(x_own, x_oth, dg_own, dg_oth, *parts):
    row = lax.broadcasted_iota(jnp.int32, (128, 2 * ROWS), 0)
    both = lambda at: jnp.concatenate([x_own[at, :], x_oth[at, :]], axis=1)
    for r in range(2):
        d_all = jnp.concatenate([dg_own[r], dg_oth[r]], axis=1)
        edge = d_all[768:896]
        none = jnp.zeros_like(edge)
        edge = jnp.concatenate([jnp.where(row < 96, edge, none), jnp.where(row < 96, none, edge)], axis=1)
        for s in range(0, 8, 8 // CUTS):
            rows = D // CUTS
            hid = both(slice(144 * s, 144 * s + rows))
            attn = both(slice(D + 144 * s, D + 144 * s + rows))
            pieces = [
                (0, mm(hid, d_all[:384], NT)),
                (384, mm(hid, d_all[384:768], NT)),
                (768, mm(jnp.concatenate([hid, attn], axis=1), edge, NT)),
                (896, mm(attn, d_all[896:], NT)),
            ]
            for lo, piece in pieces:
                cols = slice(lo, lo + piece.shape[1])
                piece = piece.astype(BF)
                for t in range(8 // CUTS):
                    part = piece[144 * t : 144 * (t + 1)]
                    if s + t < 4:
                        parts[s + t][r, :, cols] = part
                    else:
                        ra, half = divmod(s + t - 4, 2)
                        parts[4 + 2 * ra + r][144 * half : 144 * (half + 1), cols] = part


def shape(*dims, dtype=BF):
    return jax.ShapeDtypeStruct(dims, dtype)


def call(kernel, outs, ins, flops, mib, scratch=(), specs=None):
    return pl.pallas_call(
        kernel,
        out_shape=outs,
        in_specs=specs or [VMEM] * len(ins),
        out_specs=[VMEM] * len(outs) if isinstance(outs, list) else ANY,
        scratch_shapes=list(scratch),
        compiler_params=pltpu.CompilerParams(vmem_limit_bytes=mib * MIB),
        cost_estimate=pl.CostEstimate(flops=flops, bytes_accessed=10**7, transcendentals=0),
    )(*ins)


def prepare_call(place, w_qkv, w_out):
    return call(
        prepare_kernel,
        shape(14 * D, D),
        (place, w_qkv, w_out),
        10**9,
        32,
        scratch=[pltpu.VMEM((3, D, D), BF), pltpu.VMEM((5 * D, D), BF), pltpu.SemaphoreType.DMA((5,))],
        specs=[SMEM, ANY, ANY],
    )


def attend_call(place, both, prepared):
    return call(
        attend_kernel,
        [shape(2 * D, ROWS), shape(2, D, ROWS), shape(2, D, ROWS)],
        (place, both, prepared),
        10 * 10**9,
        28,
        scratch=[
            pltpu.VMEM((5, D, D), BF),
            pltpu.SemaphoreType.DMA((5,)),
            pltpu.VMEM((3 * D, ROWS), F32),
            pltpu.VMEM((D, ROWS), F32),
            pltpu.VMEM((3 * D, ROWS), F32),
            pltpu.VMEM((D, ROWS), F32),
        ],
        specs=[SMEM, VMEM, ANY],
    )


def total(own, others):
    return own.astype(F32) + sum(g.astype(F32) for g in others)


def per_device(hidden_in, grad_out, w_qkv, w_out):
    place = jnp.stack([lax.axis_index(a) for a in ("x", "z", "yh", "yl", "c")]).astype(jnp.int32)
    both = call(
        pack_kernel,
        shape(512, D),
        (hidden_in.reshape(ROWS, D), grad_out.reshape(ROWS, D)),
        10**9,
        58,
        scratch=[pltpu.VMEM((2, ROWS, D), BF), pltpu.VMEM((512, D), BF), pltpu.SemaphoreType.DMA((4,))],
        specs=[ANY, ANY],
    )
    both = lax.all_to_all(both, FRAME, split_axis=0, concat_axis=0, tiled=True)
    prepared = prepare_call(place, w_qkv, w_out)
    x_own, dg_own, dg_other = attend_call(place, both, prepared)
    x_oth, dg_oth = flip(x_own, "c", 1), flip(dg_other, "c", 1)
    parts = call(
        product_kernel,
        [shape(2, 144, D)] * 4 + [shape(288, D)] * 4,
        (x_own, x_oth, dg_own, dg_oth),
        6 * 10**9,
        20,
    )
    part_a, part_b = parts[:4], parts[4:]
    got_a, got_b = [], []
    for i, s in enumerate((1, 2, 3)):
        got_a.append(flip(part_a[s], "x", s))
        got_b.append(flip(part_b[(2, 1, 3)[i]], Y, (2, 1, 3)[i]))

    dg_own, dg_other, _ = lax.optimization_barrier((dg_own, dg_other, got_a[0]))
    grad_in = call(
        grad_in_kernel,
        shape(512, 640),
        (place, dg_own, dg_other, prepared),
        3 * 10**9,
        20,
        scratch=[pltpu.VMEM((4, 864, D), BF), pltpu.VMEM((512, 640), BF), pltpu.SemaphoreType.DMA((5,))],
        specs=[SMEM, VMEM, VMEM, ANY],
    )

    sum_a = total(part_a[0], got_a).astype(BF).reshape(2, 2, 72, D)
    sum_b = total(part_b[0], got_b).astype(BF).reshape(4, 72, D)
    got_a, got_b = [], []
    for s in (2, 1, 3):
        got_a.append(flip(sum_a[s & 1, s >> 1], Y, s))
        got_b.append(flip(sum_b[s], "x", s))
    sum_a = total(sum_a[0, 0], got_a).reshape(4, 18, D)
    sum_b = total(sum_b[0], got_b).reshape(4, 18, D)
    got = [flip(jnp.concatenate([sum_a[i], sum_b[i]]).astype(BF), "z", s) for i, s in ((2, 6), (3, 7), (1, 1))]
    near = total(sum_a[0], [g[:18] for g in got])
    grad_in = lax.all_to_all(grad_in, FRAME, split_axis=0, concat_axis=0, tiled=True)
    (grad_in,) = call(unpack_kernel, [shape(ROWS, D)], (grad_in,), 10**9, 16)
    near, grad_in = lax.optimization_barrier((near, grad_in))
    far = flip(total(sum_b[0], [g[18:] for g in got]).astype(BF), "z", 2)
    grad_wqkv = total(near[:, :864], [far[:, :864]])
    grad_wout = total(near[:, 864:], [far[:, 864:]])
    return grad_in.reshape(2, 128, D), grad_wqkv, grad_wout


def solution(mesh):
    fine = Mesh(mesh.devices.reshape(4, 8, 2, 2, 2), ("x", "z", "yh", "yl", "c"))
    patch = ("yl", "c")
    in_specs = (P(FRAME, patch, None), P(FRAME, patch, None), P(), P())
    out_specs = (P(FRAME, patch, None), P(FRAME, patch), P(FRAME, patch))
    return jax.shard_map(
        per_device, mesh=fine, in_specs=in_specs, out_specs=out_specs, check_vma=False
    )
```
